32 devices in a mesh: blk: 16 (over z, y, x), mc: 2 (over core).
Axes of the slice: x: 2, y: 2, z: 4, core: 2. Of those that a mesh axis runs over, the one named last changes fastest.
Arguments:
- batch_ids: int32 [512], P('blk'), may hold values from 0 to 4095, as said below
- cond_ids: int32 [512, 3], P('blk'), may hold values from 0 to 4095, as said below
- home: int32 [4096], replicated, may hold values from 0 to 4095, as said below
- latent: bfloat16 [4096, 32, 256], P('blk', 'mc'), may hold values from -6 to 6
- diag_factor: bfloat16 [512, 256, 256], P('blk'), may hold values from -0.375 to 0.375
- cond_factor: bfloat16 [512, 3, 256, 256], P('blk'), may hold values from -0.375 to 0.375
- obs: float32 [512, 256], P('blk'), may hold values from -6 to 6
- noise_prec: float32 [], replicated, may hold values from 0.5 to 2
Outputs:
- mean_grad: float32 [4096, 256], P('blk', 'mc')
The draws below stay inside these ranges and needn't reach their ends.
Inputs may be any that keep to these rules, and one draw needn't show every extreme that they name: home is a permutation; block b is stored at position home[b], on index home[b] // 256 of blk. `batch_ids`: of the 128 blocks named by one index's rows (each row's own block and its conditioning blocks, repeats counted), at most 20 are stored on any one index of blk. `cond_ids`: counted together with batch_ids as stated there.
All inputs are finite; a program needn't handle non-finite values.
Results may differ from the reference program's by a relative error of at most 0.0029.
Values may be sent and summed in bfloat16 or wider, within the bound.
A program may use at most 64 MiB of HBM per device.

```python
import math
import jax
import jax.numpy as jnp
from jax import lax

BLOCK = 256
COND = 3
ROWS_DEV = 32
OWNED = 256
DRAWS = 32
ROWS = 512
BLOCKS = 4096
CAPACITY = 20


def request_plan(base_key):
    owners = BLOCKS // OWNED
    want_count = 4 * ROWS_DEV
    pool_size = owners * CAPACITY
    home_perm = jax.random.permutation(jax.random.fold_in(base_key, 11), BLOCKS).astype(jnp.int32)
    inverse_home = jnp.argsort(home_perm).astype(jnp.int32)
    hot_owner = jax.random.randint(jax.random.fold_in(base_key, 12), (), 0, owners)
    pool_owner = jnp.arange(pool_size, dtype=jnp.int32) // CAPACITY
    order_key = jnp.arange(pool_size, dtype=jnp.int32)
    scores = jax.random.randint(jax.random.fold_in(base_key, 13), (owners, pool_size), 0, 1 << 20) * pool_size + order_key[None, :]
    scores = jnp.where(pool_owner[None, :] == hot_owner, order_key[None, :] - pool_size, scores)
    chosen = jnp.argsort(scores, axis=1)[:, :want_count]
    dest_dev = pool_owner[chosen]
    mix_scores = jax.random.randint(jax.random.fold_in(base_key, 14), (owners, want_count), 0, 1 << 20) * want_count + jnp.arange(want_count, dtype=jnp.int32)[None, :]
    mixing = jnp.argsort(mix_scores, axis=1)
    dest_dev = jnp.take_along_axis(dest_dev, mixing, axis=1)
    slot_idx = jax.random.randint(jax.random.fold_in(base_key, 15), (owners, want_count), 0, OWNED)
    position = (dest_dev * OWNED + slot_idx).reshape(-1)
    block_ids = inverse_home[position].reshape(owners * ROWS_DEV, 4).astype(jnp.int32)
    return (home_perm, block_ids)


def draw_batch_ids(key, part):
    home_perm, block_ids = request_plan(key)
    return block_ids[:, 0]


def draw_cond_ids(key, part):
    home_perm, block_ids = request_plan(key)
    return block_ids[:, 1:]


def draw_home(key, part):
    home_perm, block_ids = request_plan(key)
    return home_perm


def level_of(own_key, extent, pieces, least, high):
    def one(dim, parts):
        steps = jax.random.uniform(jax.random.fold_in(jax.random.fold_in(own_key, 6), dim), (parts,), jnp.float32, least / len(pieces), high / len(pieces))
        return jnp.repeat(jnp.exp(steps), extent[dim] // parts).reshape((-1,) + (1,) * (len(extent) - dim - 1))

    gain = one(*pieces[0])
    for cut in pieces[1:]:
        gain = gain * one(*cut)
    return gain


def scatter_about(rng, dims, spread, reach, split=(), kind=jnp.bfloat16):
    array = spread * jax.random.normal(rng, dims, jnp.float32)
    if split:
        array = array * level_of(rng, dims, split, -0.22, 0.18)
    return jnp.clip(array, -reach, reach).astype(kind)


def setup_inputs(seed: int = 0) -> dict:
    arg_keys = jax.random.split(jax.random.key(seed), 9)
    return {
        "batch_ids": draw_batch_ids(jax.random.fold_in(arg_keys[8], 71), 0),
        "cond_ids": draw_cond_ids(jax.random.fold_in(arg_keys[8], 71), 0),
        "home": draw_home(jax.random.fold_in(arg_keys[8], 71), 0),
        "latent": scatter_about(arg_keys[3], (BLOCKS, DRAWS, BLOCK), 1.0, 6.0, ((0, 16), (1, 2))),
        "diag_factor": scatter_about(arg_keys[4], (ROWS, BLOCK, BLOCK), BLOCK ** -0.5, 0.375, ((0, 16),)),
        "cond_factor": scatter_about(arg_keys[5], (ROWS, COND, BLOCK, BLOCK), BLOCK ** -0.5, 0.375, ((0, 16),)),
        "obs": scatter_about(arg_keys[6], (ROWS, BLOCK), 1.0, 6.0, ((0, 16),), jnp.float32),
        "noise_prec": jnp.clip(jnp.exp(jax.random.uniform(arg_keys[7], (), jnp.float32, math.log(0.5), math.log(2.0))), 0.5, 2.0),
    }


freedom = 4.0


def reference(batch_ids, cond_ids, home, latent, diag_factor, cond_factor, obs, noise_prec):
    own_where = home[batch_ids].astype(jnp.int32)
    cond_where = home[cond_ids].astype(jnp.int32)
    lower_mask = jnp.arange(BLOCK)[:, None] >= jnp.arange(BLOCK)[None, :]
    inverse_draws = 1.0 / DRAWS

    def one_row(packed):
        own_pos, near_pos, diag_block, cond_blocks, seen = packed
        own_panel = latent[own_pos]
        lower_diag = jnp.where(lower_mask, diag_block, jnp.zeros_like(diag_block))
        whitened = jnp.dot(own_panel, lower_diag.T, preferred_element_type=jnp.float32)
        for which in range(COND):
            near_panel = latent[near_pos[which]]
            whitened = whitened + jnp.dot(near_panel, cond_blocks[which].T, preferred_element_type=jnp.float32)
        scored = (freedom + 1.0) * whitened / (freedom + whitened * whitened)
        white_low = scored.astype(jnp.bfloat16)
        back_diag = jnp.dot(white_low, lower_diag, preferred_element_type=jnp.float32)
        likely = noise_prec * (seen[None, :] - own_panel.astype(jnp.float32))
        self_term = jnp.sum(likely - back_diag, axis=0) * inverse_draws
        cond_list = []
        for which in range(COND):
            back_cond = jnp.dot(white_low, cond_blocks[which], preferred_element_type=jnp.float32)
            cond_list.append(-jnp.sum(back_cond, axis=0) * inverse_draws)
        return self_term, jnp.stack(cond_list)

    self_terms, cond_terms = lax.map(one_row, (own_where, cond_where, diag_factor, cond_factor, obs))
    mean_grad = jnp.zeros((BLOCKS, BLOCK), jnp.float32)
    mean_grad = mean_grad.at[own_where].add(self_terms)
    mean_grad = mean_grad.at[cond_where.reshape(-1)].add(cond_terms.reshape(-1, BLOCK))
    return mean_grad
```

```python
import functools

import jax
import jax.numpy as jnp
from jax import lax
from jax.experimental import pallas as pl
from jax.experimental.pallas import tpu as pltpu
from jax.sharding import PartitionSpec as P

freedom = 4.0
MESH = pl.DeviceIdType.MESH
f32 = jnp.float32
bf16 = jnp.bfloat16
NT = (((1,), (1,)), ((), ()))


def kernel(
    n,
    cap,
    in_slots,
    pick,
    inverse,
    target,
    noise,
    latent,
    diag,
    cond,
    obs,
    out,
    outgoing,
    fetched,
    lower,
    near,
    sums,
    sums_in,
    terms,
    outbox,
    inbox,
    load_sem,
    lat_send,
    lat_recv,
    pair_sem,
    term_send,
    term_recv,
):
    rows = obs.shape[0]
    draws = latent.shape[1]
    width = latent.shape[2]
    half = width // 2
    pad = outbox.shape[1]
    me = lax.axis_index("blk")
    core = lax.axis_index("mc")
    partner = (me, 1 - core)
    inverse_draws = 1.0 / (2 * draws)

    load_diag = pltpu.make_async_copy(diag, lower, load_sem.at[0])
    load_cond = pltpu.make_async_copy(cond, near, load_sem.at[1])
    load_diag.start()
    load_cond.start()

    barrier = pltpu.get_barrier_semaphore()

    @pl.loop(1, n)
    def _(o):
        pl.semaphore_signal(
            barrier, inc=1, device_id=(lax.rem(me + o, n), core), device_id_type=MESH
        )

    pl.semaphore_signal(barrier, inc=1, device_id=partner, device_id_type=MESH)
    pl.semaphore_wait(barrier, n)

    def latent_copy(o):
        dst = lax.rem(me + o, n)
        return pltpu.make_async_remote_copy(
            src_ref=outgoing.at[dst],
            dst_ref=fetched.at[pl.ds(me * cap, cap)],
            send_sem=lat_send.at[o],
            recv_sem=lat_recv.at[o],
            device_id=(dst, core),
            device_id_type=MESH,
        )

    @pl.loop(1, n)
    def _(o):
        dst = lax.rem(me + o, n)
        for c in range(cap):
            outgoing[dst, c] = latent[in_slots[dst * cap + c]]
        latent_copy(o).start()

    for c in range(cap):
        fetched[me * cap + c] = latent[in_slots[me * cap + c]]

    outbox[...] = jnp.zeros_like(outbox)
    load_diag.wait()
    keep = lax.broadcasted_iota(jnp.int32, (width, width), 0) >= lax.broadcasted_iota(
        jnp.int32, (width, width), 1
    )

    @pl.loop(0, rows)
    def _(r):
        lower[r] = jnp.where(keep, lower[r], jnp.zeros((width, width), bf16))

    load_cond.wait()

    @pl.loop(1, n)
    def _(o):
        latent_copy(o).wait_recv()

    @pl.loop(0, rows, unroll=2)
    def _(r):
        own = fetched[pick[4 * r]]
        white = lax.dot_general(own, lower[r], NT, preferred_element_type=f32)
        for k in range(3):
            panel = fetched[pick[4 * r + k + 1]]
            white = white + lax.dot_general(panel, near[r, k], NT, preferred_element_type=f32)
        scored = (freedom + 1.0) * white / (freedom + white * white)
        low = scored.astype(bf16).astype(f32)
        sums[pl.ds(r, 1)] = jnp.sum(low, axis=0, keepdims=True)
        sums[pl.ds(rows + r, 1)] = jnp.sum(own.astype(f32), axis=0, keepdims=True)

    swap = pltpu.make_async_remote_copy(
        src_ref=sums,
        dst_ref=sums_in,
        send_sem=pair_sem.at[0],
        recv_sem=pair_sem.at[1],
        device_id=partner,
        device_id_type=MESH,
    )
    swap.start()
    swap.wait()
    sums_in[...] = sums_in[...] + sums[...]

    column = pl.ds(pl.multiple_of(core * half, half), half)
    place = lax.broadcasted_iota(jnp.int32, (16, width), 0)

    @pl.loop(0, rows, unroll=2)
    def _(r):
        total = jnp.broadcast_to(sums_in[pl.ds(r, 1)], (16, width))
        high = total.astype(bf16).astype(f32)
        parts = jnp.where(place == 0, high, jnp.where(place == 1, total - high, 0.0)).astype(bf16)
        back = jnp.dot(parts, lower[r, :, column], preferred_element_type=f32)
        back = jnp.sum(back, axis=0, keepdims=True)
        likely = noise[0] * (2 * draws * obs[pl.ds(r, 1)] - sums_in[pl.ds(rows + r, 1)])
        likely = jnp.where(core == 0, likely[:, :half], likely[:, half:])
        terms[pl.ds(4 * r, 1)] = (likely - back) * inverse_draws
        for k in range(3):
            back = jnp.dot(parts, near[r, k, :, column], preferred_element_type=f32)
            back = jnp.sum(back, axis=0, keepdims=True)
            terms[pl.ds(4 * r + k + 1, 1)] = -back * inverse_draws

    def term_copy(o):
        dst = lax.rem(me + o, n)
        return pltpu.make_async_remote_copy(
            src_ref=outbox.at[dst],
            dst_ref=inbox.at[me],
            send_sem=term_send.at[o],
            recv_sem=term_recv.at[o],
            device_id=(dst, core),
            device_id_type=MESH,
        )

    @pl.loop(1, n)
    def _(o):
        dst = lax.rem(me + o, n)
        for c in range(cap):
            outbox[dst, pl.ds(c, 1)] = terms[pl.ds(inverse[dst * cap + c], 1)]
        term_copy(o).start()

    for c in range(cap):
        outbox[me, pl.ds(c, 1)] = terms[pl.ds(inverse[me * cap + c], 1)]
    inbox[me] = outbox[me]

    slots = out.shape[0]
    hits = lax.broadcasted_iota(jnp.int32, (slots, n * pad), 0) == target[...]
    hits = jnp.where(hits, 1.0, 0.0).astype(bf16)

    @pl.loop(1, n)
    def _(o):
        term_copy(o).wait_recv()

    arrived = inbox[...].reshape(n * pad, half)
    first = arrived.astype(bf16)
    rest = arrived - first.astype(f32)
    second = rest.astype(bf16)
    third = (rest - second.astype(f32)).astype(bf16)
    total = jnp.dot(hits, first, preferred_element_type=f32)
    total = total + jnp.dot(hits, second, preferred_element_type=f32)
    out[...] = total + jnp.dot(hits, third, preferred_element_type=f32)

    @pl.loop(1, n)
    def _(o):
        latent_copy(o).wait_send()
        term_copy(o).wait_send()


def body(batch_ids, cond_ids, home, latent, diag_factor, cond_factor, obs, noise_prec):
    n = lax.axis_size("blk")
    me = lax.axis_index("blk")
    per_owner, draws, width = latent.shape
    rows = batch_ids.shape[0]
    want = 4 * rows
    cap = max(2, 10 * rows // n)
    pad = -(-cap // 8) * 8
    block_ids = jnp.concatenate([batch_ids[:, None], cond_ids], axis=1).reshape(-1)
    wanted = home[block_ids]
    every = lax.all_gather(wanted, "blk")
    rank_of = jnp.arange(cap)

    before = jnp.arange(want)[:, None] < jnp.arange(want)[None, :]
    mine = every // per_owner == me
    rank = jnp.dot(mine.astype(bf16), before.astype(bf16), preferred_element_type=f32)
    rank = jnp.where(mine, rank.astype(jnp.int32), -1)
    hit = rank[:, None, :] == rank_of[None, :, None]
    in_slots = jnp.sum(jnp.where(hit, (every % per_owner + 1)[:, None, :], 0), axis=2) - 1
    target = jnp.pad(in_slots, ((0, 0), (0, pad - cap)), constant_values=-1).reshape(1, n * pad)

    owner = wanted // per_owner
    same = owner[:, None] == owner[None, :]
    own_rank = jnp.sum((same & before).astype(jnp.int32), axis=0)
    pick = owner * cap + own_rank
    spot = jnp.arange(n * cap)
    inverse = jnp.sum(
        jnp.where(pick[None, :] == spot[:, None], jnp.arange(want)[None, :], 0), axis=1
    )

    smem = pl.BlockSpec(memory_space=pltpu.SMEM)
    vmem = pl.BlockSpec(memory_space=pltpu.VMEM)
    anywhere = pl.BlockSpec(memory_space=pl.ANY)
    return pl.pallas_call(
        functools.partial(kernel, n, cap),
        out_shape=jax.ShapeDtypeStruct((per_owner, width // 2), f32),
        in_specs=[smem, smem, smem, vmem, smem, vmem, anywhere, anywhere, vmem],
        out_specs=vmem,
        scratch_shapes=[
            pltpu.VMEM((n, cap, draws, width), bf16),
            pltpu.VMEM((n * cap, draws, width), bf16),
            pltpu.VMEM(diag_factor.shape, bf16),
            pltpu.VMEM(cond_factor.shape, bf16),
            pltpu.VMEM((2 * rows, width), f32),
            pltpu.VMEM((2 * rows, width), f32),
            pltpu.VMEM((want, width // 2), f32),
            pltpu.VMEM((n, pad, width // 2), f32),
            pltpu.VMEM((n, pad, width // 2), f32),
            pltpu.SemaphoreType.DMA((2,)),
            pltpu.SemaphoreType.DMA((n,)),
            pltpu.SemaphoreType.DMA((n,)),
            pltpu.SemaphoreType.DMA((2,)),
            pltpu.SemaphoreType.DMA((n,)),
            pltpu.SemaphoreType.DMA((n,)),
        ],
        compiler_params=pltpu.CompilerParams(
            collective_id=0, has_side_effects=True, vmem_limit_bytes=56 * 1024 * 1024
        ),
    )(
        jnp.maximum(in_slots, 0).reshape(-1),
        pick,
        inverse,
        target,
        noise_prec.reshape(1),
        latent,
        diag_factor,
        cond_factor,
        obs,
    )


def solution(mesh):
    placed = (
        P("blk"),
        P("blk", None),
        P(),
        P("blk", "mc", None),
        P("blk", None, None),
        P("blk", None, None, None),
        P("blk", None),
        P(),
    )
    return jax.shard_map(
        body, mesh=mesh, in_specs=placed, out_specs=P("blk", "mc"), check_vma=False
    )
```

```python
import functools

import jax
import jax.numpy as jnp
from jax import lax
from jax.experimental import pallas as pl
from jax.experimental.pallas import tpu as pltpu
from jax.sharding import PartitionSpec as P

freedom = 4.0
MESH = pl.DeviceIdType.MESH
f32 = jnp.float32
bf16 = jnp.bfloat16
NT = (((1,), (1,)), ((), ()))


def kernel(
    n,
    cap,
    wanted,
    noise,
    latent_any,
    diag,
    cond,
    obs,
    out,
    every,
    tables,
    scalars,
    latent,
    outgoing,
    fetched_left,
    fetched_right,
    lower,
    near,
    partial,
    sums,
    sums_in,
    terms,
    outbox,
    inbox,
    load_sem,
    id_send,
    id_recv,
    lat_send,
    lat_recv,
    pair_sem,
    term_send,
    term_recv,
):
    fetched = (fetched_left, fetched_right)
    rows = obs.shape[0]
    want = 4 * rows
    per_owner, draws, width = latent.shape
    half = width // 2
    me = lax.axis_index("blk")
    core = lax.axis_index("mc")
    partner = (me, 1 - core)
    inverse_draws = 1.0 / (2 * draws)

    load_latent = pltpu.make_async_copy(latent_any, latent, load_sem.at[2])
    load_diag = pltpu.make_async_copy(diag, lower, load_sem.at[0])
    load_cond = pltpu.make_async_copy(cond, near, load_sem.at[1])
    load_latent.start()
    load_diag.start()
    load_cond.start()

    barrier = pltpu.get_barrier_semaphore()

    @pl.loop(1, n)
    def _(o):
        pl.semaphore_signal(
            barrier, inc=1, device_id=(lax.rem(me + o, n), core), device_id_type=MESH
        )

    pl.semaphore_signal(barrier, inc=1, device_id=partner, device_id_type=MESH)
    pl.semaphore_wait(barrier, n)

    def id_copy(o):
        return pltpu.make_async_remote_copy(
            src_ref=wanted,
            dst_ref=every.at[me],
            send_sem=id_send.at[o],
            recv_sem=id_recv.at[o],
            device_id=(lax.rem(me + o, n), core),
            device_id_type=MESH,
        )

    @pl.loop(1, n)
    def _(o):
        id_copy(o).start()

    every[me] = wanted[...]
    lane = lax.broadcasted_iota(jnp.int32, (n, want), 1)
    owner = lax.broadcasted_iota(jnp.int32, (n, want), 0)

    def ranks(mask):
        count = jnp.where(mask, 1, 0)
        shift = 1
        while shift < want:
            count = count + jnp.where(lane >= shift, pltpu.roll(count, shift, 1), 0)
            shift *= 2
        return count - 1

    def table(mask, rank, value):
        rank = jnp.where(mask, rank, -1)
        filled = jnp.zeros((n, want), jnp.int32)
        for c in range(cap):
            found = jnp.sum(jnp.where(rank == c, value, 0), axis=1, keepdims=True)
            filled = jnp.where(lane == c, found, filled)
        return filled

    mine = jnp.broadcast_to(wanted[...], (n, want)) - owner * per_owner
    mine = (mine >= 0) & (mine < per_owner)
    rank = ranks(mine)
    tables[pl.ds(n, n)] = table(mine, rank, lane)
    spot = jnp.sum(jnp.where(mine, owner * cap + rank, 0), axis=0, keepdims=True)
    tables[pl.ds(2 * n, 8)] = jnp.broadcast_to(spot, (8, want))

    @pl.loop(1, n)
    def _(o):
        id_copy(o).wait_recv()

    slot = every[...].reshape(n, want) - me * per_owner
    mine = (slot >= 0) & (slot < per_owner)
    tables[pl.ds(0, n)] = table(mine, ranks(mine), slot + 1) - 1
    to_scalars = pltpu.make_async_copy(tables, scalars, load_sem.at[3])
    to_scalars.start()
    load_latent.wait()
    to_scalars.wait()

    def slot_of(owner, c):
        return jnp.maximum(scalars[owner, c], 0)

    def term_of(owner, c):
        return scalars[n + owner, c]

    def panel_of(w):
        return scalars[2 * n, w]

    def latent_copy(h, o):
        dst = lax.rem(me + o, n)
        return pltpu.make_async_remote_copy(
            src_ref=outgoing.at[h, dst],
            dst_ref=fetched[h].at[pl.ds(me * cap, cap)],
            send_sem=lat_send.at[h * n + o],
            recv_sem=lat_recv.at[h * n + o],
            device_id=(dst, core),
            device_id_type=MESH,
        )

    for h in range(2):
        part = slice(h * half, (h + 1) * half)

        @pl.loop(1, n)
        def _(o):
            dst = lax.rem(me + o, n)
            for c in range(cap):
                outgoing[h, dst, c] = latent[slot_of(dst, c), :, part]
            latent_copy(h, o).start()

    for h in range(2):
        part = slice(h * half, (h + 1) * half)
        for c in range(cap):
            fetched[h][me * cap + c] = latent[slot_of(me, c), :, part]

    outbox[...] = jnp.zeros_like(outbox)
    load_diag.wait()
    keep = lax.broadcasted_iota(jnp.int32, (width, width), 0) >= lax.broadcasted_iota(
        jnp.int32, (width, width), 1
    )

    @pl.loop(0, rows)
    def _(r):
        lower[r] = jnp.where(keep, lower[r], jnp.zeros((width, width), bf16))

    load_cond.wait()

    def product(h, r):
        part = slice(h * half, (h + 1) * half)
        panels = [fetched[h][panel_of(4 * r + k)] for k in range(4)]
        blocks = [lower[r, :, part]] + [near[r, k, :, part] for k in range(3)]
        return lax.dot_general(
            jnp.concatenate(panels, axis=1),
            jnp.concatenate(blocks, axis=1),
            NT,
            preferred_element_type=f32,
        )

    @pl.loop(1, n)
    def _(o):
        latent_copy(0, o).wait_recv()

    @pl.loop(0, rows, unroll=4)
    def _(r):
        partial[r] = product(0, r)

    @pl.loop(1, n)
    def _(o):
        latent_copy(1, o).wait_recv()

    @pl.loop(0, rows, unroll=4)
    def _(r):
        white = partial[r] + product(1, r)
        scored = (freedom + 1.0) * white / (freedom + white * white)
        low = scored.astype(bf16).astype(f32)
        sums[pl.ds(r, 1)] = jnp.sum(low, axis=0, keepdims=True)
        spot = panel_of(4 * r)
        own = jnp.concatenate([fetched_left[spot], fetched_right[spot]], axis=1).astype(f32)
        sums[pl.ds(rows + r, 1)] = jnp.sum(own, axis=0, keepdims=True)

    swap = pltpu.make_async_remote_copy(
        src_ref=sums,
        dst_ref=sums_in,
        send_sem=pair_sem.at[0],
        recv_sem=pair_sem.at[1],
        device_id=partner,
        device_id_type=MESH,
    )
    swap.start()
    swap.wait()
    sums_in[...] = sums_in[...] + sums[...]

    column = pl.ds(pl.multiple_of(core * half, half), half)
    place = lax.broadcasted_iota(jnp.int32, (16, width), 0)

    @pl.loop(0, rows, unroll=4)
    def _(r):
        total = jnp.broadcast_to(sums_in[pl.ds(r, 1)], (16, width))
        high = total.astype(bf16).astype(f32)
        parts = jnp.where(place == 0, high, jnp.where(place == 1, total - high, 0.0)).astype(bf16)
        back = jnp.dot(parts, lower[r, :, column], preferred_element_type=f32)
        back = jnp.sum(back, axis=0, keepdims=True)
        likely = noise[0] * (2 * draws * obs[pl.ds(r, 1)] - sums_in[pl.ds(rows + r, 1)])
        likely = jnp.where(core == 0, likely[:, :half], likely[:, half:])
        terms[pl.ds(4 * r, 1)] = (likely - back) * inverse_draws
        for k in range(3):
            back = jnp.dot(parts, near[r, k, :, column], preferred_element_type=f32)
            back = jnp.sum(back, axis=0, keepdims=True)
            terms[pl.ds(4 * r + k + 1, 1)] = -back * inverse_draws

    def term_copy(o):
        dst = lax.rem(me + o, n)
        return pltpu.make_async_remote_copy(
            src_ref=outbox.at[dst],
            dst_ref=inbox.at[me],
            send_sem=term_send.at[o],
            recv_sem=term_recv.at[o],
            device_id=(dst, core),
            device_id_type=MESH,
        )

    @pl.loop(1, n)
    def _(o):
        dst = lax.rem(me + o, n)
        for c in range(cap):
            outbox[dst, pl.ds(c, 1)] = terms[pl.ds(term_of(dst, c), 1)]
        term_copy(o).start()

    for c in range(cap):
        outbox[me, pl.ds(c, 1)] = terms[pl.ds(term_of(me, c), 1)]
    inbox[me] = outbox[me]
    pad = outbox.shape[1]
    place = lax.broadcasted_iota(jnp.int32, (per_owner, want), 0)

    def collect(source):
        hits = jnp.where(place == tables[pl.ds(source, 1)], 1.0, 0.0).astype(bf16)[:, :pad]
        arrived = inbox[source]
        first = arrived.astype(bf16)
        rest = arrived - first.astype(f32)
        second = rest.astype(bf16)
        third = (rest - second.astype(f32)).astype(bf16)
        total = jnp.dot(hits, first, preferred_element_type=f32)
        total = total + jnp.dot(hits, second, preferred_element_type=f32)
        return total + jnp.dot(hits, third, preferred_element_type=f32)

    out[...] = collect(me)

    @pl.loop(1, n)
    def _(o):
        term_copy(o).wait_recv()
        out[...] += collect(lax.rem(me - o + n, n))

    @pl.loop(1, n)
    def _(o):
        id_copy(o).wait_send()
        latent_copy(0, o).wait_send()
        latent_copy(1, o).wait_send()
        term_copy(o).wait_send()


def body(batch_ids, cond_ids, home, latent, diag_factor, cond_factor, obs, noise_prec):
    n = lax.axis_size("blk")
    per_owner, draws, width = latent.shape
    rows = batch_ids.shape[0]
    want = 4 * rows
    cap = max(2, 10 * rows // n)
    pad = -(-cap // 8) * 8
    block_ids = jnp.concatenate([batch_ids[:, None], cond_ids], axis=1).reshape(-1)
    wanted = home[block_ids].reshape(1, want)

    smem = pl.BlockSpec(memory_space=pltpu.SMEM)
    vmem = pl.BlockSpec(memory_space=pltpu.VMEM)
    anywhere = pl.BlockSpec(memory_space=pl.ANY)
    return pl.pallas_call(
        functools.partial(kernel, n, cap),
        out_shape=jax.ShapeDtypeStruct((per_owner, width // 2), f32),
        in_specs=[vmem, smem, anywhere, anywhere, anywhere, vmem],
        out_specs=vmem,
        scratch_shapes=[
            pltpu.VMEM((n, 1, want), jnp.int32),
            pltpu.VMEM((2 * n + 8, want), jnp.int32),
            pltpu.SMEM((2 * n + 8, want), jnp.int32),
            pltpu.VMEM(latent.shape, bf16),
            pltpu.VMEM((2, n, cap, draws, width // 2), bf16),
            pltpu.VMEM((n * cap, draws, width // 2), bf16),
            pltpu.VMEM((n * cap, draws, width // 2), bf16),
            pltpu.VMEM(diag_factor.shape, bf16),
            pltpu.VMEM(cond_factor.shape, bf16),
            pltpu.VMEM((rows, draws, width), f32),
            pltpu.VMEM((2 * rows, width), f32),
            pltpu.VMEM((2 * rows, width), f32),
            pltpu.VMEM((want, width // 2), f32),
            pltpu.VMEM((n, pad, width // 2), f32),
            pltpu.VMEM((n, pad, width // 2), f32),
            pltpu.SemaphoreType.DMA((4,)),
            pltpu.SemaphoreType.DMA((n,)),
            pltpu.SemaphoreType.DMA((n,)),
            pltpu.SemaphoreType.DMA((2 * n,)),
            pltpu.SemaphoreType.DMA((2 * n,)),
            pltpu.SemaphoreType.DMA((2,)),
            pltpu.SemaphoreType.DMA((n,)),
            pltpu.SemaphoreType.DMA((n,)),
        ],
        compiler_params=pltpu.CompilerParams(
            collective_id=0, has_side_effects=True, vmem_limit_bytes=56 * 1024 * 1024
        ),
    )(wanted, noise_prec.reshape(1), latent, diag_factor, cond_factor, obs)


def solution(mesh):
    placed = (
        P("blk"),
        P("blk", None),
        P(),
        P("blk", "mc", None),
        P("blk", None, None),
        P("blk", None, None, None),
        P("blk", None),
        P(),
    )
    return jax.shard_map(
        body, mesh=mesh, in_specs=placed, out_specs=P("blk", "mc"), check_vma=False
    )
```

```python
import functools

import jax
import jax.numpy as jnp
from jax import lax
from jax.experimental import pallas as pl
from jax.experimental.pallas import tpu as pltpu
from jax.sharding import PartitionSpec as P

freedom = 4.0
MESH = pl.DeviceIdType.MESH
f32 = jnp.float32
bf16 = jnp.bfloat16
NT = (((1,), (1,)), ((), ()))


def kernel(
    n,
    cap,
    wanted,
    noise,
    latent_any,
    diag,
    cond,
    obs,
    out,
    every,
    tables,
    scalars,
    latent,
    outgoing,
    fetched_left,
    fetched_right,
    lower,
    near,
    partial,
    sums,
    sums_in,
    terms,
    outbox,
    inbox,
    load_sem,
    id_send,
    id_recv,
    lat_send,
    lat_recv,
    pair_sem,
    term_send,
    term_recv,
):
    fetched = (fetched_left, fetched_right)
    rows = obs.shape[0]
    want = 4 * rows
    per_owner, draws, width = latent.shape
    half = width // 2
    me = lax.axis_index("blk")
    core = lax.axis_index("mc")
    partner = (me, 1 - core)
    inverse_draws = 1.0 / (2 * draws)

    def peer(o):
        bit, other = 1, 0
        while bit < n:
            other = other + lax.rem(me // bit + o // bit, 2) * bit
            bit *= 2
        return other

    def turn(k):
        return lax.rem(k + 1, 2) * (n // 2) + (k + 1) // 2

    load_latent = pltpu.make_async_copy(latent_any, latent, load_sem.at[2])
    load_diag = pltpu.make_async_copy(diag, lower, load_sem.at[0])
    load_cond = pltpu.make_async_copy(cond, near, load_sem.at[1])
    load_latent.start()
    load_diag.start()
    load_cond.start()

    barrier = pltpu.get_barrier_semaphore()

    @pl.loop(1, n)
    def _(o):
        pl.semaphore_signal(
            barrier, inc=1, device_id=(peer(o), core), device_id_type=MESH
        )

    pl.semaphore_signal(barrier, inc=1, device_id=partner, device_id_type=MESH)
    pl.semaphore_wait(barrier, n)

    def id_copy(o):
        return pltpu.make_async_remote_copy(
            src_ref=wanted,
            dst_ref=every.at[me],
            send_sem=id_send.at[o],
            recv_sem=id_recv.at[o],
            device_id=(peer(o), core),
            device_id_type=MESH,
        )

    @pl.loop(1, n)
    def _(o):
        id_copy(o).start()

    every[me] = wanted[...]
    lane = lax.broadcasted_iota(jnp.int32, (n, want), 1)
    owner = lax.broadcasted_iota(jnp.int32, (n, want), 0)

    def ranks(mask):
        count = jnp.where(mask, 1, 0)
        shift = 1
        while shift < want:
            count = count + jnp.where(lane >= shift, pltpu.roll(count, shift, 1), 0)
            shift *= 2
        return count - 1

    def table(mask, rank, value):
        rank = jnp.where(mask, rank, -1)
        filled = jnp.zeros((n, want), jnp.int32)
        for c in range(cap):
            found = jnp.sum(jnp.where(rank == c, value, 0), axis=1, keepdims=True)
            filled = jnp.where(lane == c, found, filled)
        return filled

    mine = jnp.broadcast_to(wanted[...], (n, want)) - owner * per_owner
    mine = (mine >= 0) & (mine < per_owner)
    rank = ranks(mine)
    tables[pl.ds(n, n)] = table(mine, rank, lane)
    spot = jnp.sum(jnp.where(mine, owner * cap + rank, 0), axis=0, keepdims=True)
    tables[pl.ds(2 * n, 8)] = jnp.broadcast_to(spot, (8, want))

    @pl.loop(1, n)
    def _(o):
        id_copy(o).wait_recv()

    slot = every[...].reshape(n, want) - me * per_owner
    mine = (slot >= 0) & (slot < per_owner)
    tables[pl.ds(0, n)] = table(mine, ranks(mine), slot + 1) - 1
    to_scalars = pltpu.make_async_copy(tables, scalars, load_sem.at[3])
    to_scalars.start()
    load_latent.wait()
    to_scalars.wait()

    def slot_of(owner, c):
        return jnp.maximum(scalars[owner, c], 0)

    def term_of(owner, c):
        return scalars[n + owner, c]

    def panel_of(w):
        return scalars[2 * n, w]

    def latent_copy(h, o):
        dst = peer(o)
        return pltpu.make_async_remote_copy(
            src_ref=outgoing.at[h, dst],
            dst_ref=fetched[h].at[pl.ds(me * cap, cap)],
            send_sem=lat_send.at[h * n + o],
            recv_sem=lat_recv.at[h * n + o],
            device_id=(dst, core),
            device_id_type=MESH,
        )

    def pack(h, o):
        dst = peer(o)
        part = slice(h * half, (h + 1) * half)
        for c in range(cap):
            outgoing[h, dst, c] = latent[slot_of(dst, c), :, part]
        latent_copy(h, o).start()

    @pl.loop(0, n - 1)
    def _(k):
        pack(0, turn(k))

    for h in range(2):
        part = slice(h * half, (h + 1) * half)
        for c in range(cap):
            fetched[h][me * cap + c] = latent[slot_of(me, c), :, part]

    outbox[...] = jnp.zeros_like(outbox)
    load_diag.wait()
    keep = lax.broadcasted_iota(jnp.int32, (width, width), 0) >= lax.broadcasted_iota(
        jnp.int32, (width, width), 1
    )

    @pl.loop(0, rows)
    def _(r):
        lower[r] = jnp.where(keep, lower[r], jnp.zeros((width, width), bf16))

    @pl.loop(0, n - 1)
    def _(k):
        latent_copy(0, turn(k)).wait_send()
        pack(1, turn(k))

    load_cond.wait()

    def product(h, r):
        part = slice(h * half, (h + 1) * half)
        panels = [fetched[h][panel_of(4 * r + k)] for k in range(4)]
        blocks = [lower[r, :, part]] + [near[r, k, :, part] for k in range(3)]
        return lax.dot_general(
            jnp.concatenate(panels, axis=1),
            jnp.concatenate(blocks, axis=1),
            NT,
            preferred_element_type=f32,
        )

    @pl.loop(1, n)
    def _(o):
        latent_copy(0, o).wait_recv()

    @pl.loop(0, rows, unroll=4)
    def _(r):
        partial[r] = product(0, r)

    @pl.loop(1, n)
    def _(o):
        latent_copy(1, o).wait_recv()

    group = rows // 2
    column = pl.ds(pl.multiple_of(core * half, half), half)
    place = lax.broadcasted_iota(jnp.int32, (16, width), 0)

    def swap(g):
        return pltpu.make_async_remote_copy(
            src_ref=sums.at[g],
            dst_ref=sums_in.at[g],
            send_sem=pair_sem.at[g],
            recv_sem=pair_sem.at[2 + g],
            device_id=partner,
            device_id_type=MESH,
        )

    for g in range(2):

        @pl.loop(0, group, unroll=4)
        def _(i):
            r = g * group + i
            white = partial[r] + product(1, r)
            scored = (freedom + 1.0) * white / (freedom + white * white)
            low = scored.astype(bf16).astype(f32)
            sums[g, pl.ds(i, 1)] = jnp.sum(low, axis=0, keepdims=True)
            spot = panel_of(4 * r)
            own = jnp.concatenate([fetched_left[spot], fetched_right[spot]], axis=1).astype(f32)
            sums[g, pl.ds(group + i, 1)] = jnp.sum(own, axis=0, keepdims=True)

        swap(g).start()

    for g in range(2):
        swap(g).wait_recv()
        sums_in[g] = sums_in[g] + sums[g]

        @pl.loop(0, group, unroll=4)
        def _(i):
            r = g * group + i
            total = jnp.broadcast_to(sums_in[g, pl.ds(i, 1)], (16, width))
            high = total.astype(bf16).astype(f32)
            parts = jnp.where(place == 0, high, jnp.where(place == 1, total - high, 0.0)).astype(bf16)
            back = jnp.dot(parts, lower[r, :, column], preferred_element_type=f32)
            back = jnp.sum(back, axis=0, keepdims=True)
            own = sums_in[g, pl.ds(group + i, 1)]
            likely = noise[0] * (2 * draws * obs[pl.ds(r, 1)] - own)
            likely = jnp.where(core == 0, likely[:, :half], likely[:, half:])
            terms[pl.ds(4 * r, 1)] = (likely - back) * inverse_draws
            for k in range(3):
                back = jnp.dot(parts, near[r, k, :, column], preferred_element_type=f32)
                back = jnp.sum(back, axis=0, keepdims=True)
                terms[pl.ds(4 * r + k + 1, 1)] = -back * inverse_draws

    def term_copy(o):
        dst = peer(o)
        return pltpu.make_async_remote_copy(
            src_ref=outbox.at[dst],
            dst_ref=inbox.at[me],
            send_sem=term_send.at[o],
            recv_sem=term_recv.at[o],
            device_id=(dst, core),
            device_id_type=MESH,
        )

    @pl.loop(0, n - 1)
    def _(k):
        o = turn(k)
        dst = peer(o)
        for c in range(cap):
            outbox[dst, pl.ds(c, 1)] = terms[pl.ds(term_of(dst, c), 1)]
        term_copy(o).start()

    for c in range(cap):
        outbox[me, pl.ds(c, 1)] = terms[pl.ds(term_of(me, c), 1)]
    inbox[me] = outbox[me]
    pad = outbox.shape[1]
    place = lax.broadcasted_iota(jnp.int32, (per_owner, want), 0)

    def collect(source):
        hits = jnp.where(place == tables[pl.ds(source, 1)], 1.0, 0.0).astype(bf16)[:, :pad]
        arrived = inbox[source]
        first = arrived.astype(bf16)
        rest = arrived - first.astype(f32)
        second = rest.astype(bf16)
        third = (rest - second.astype(f32)).astype(bf16)
        total = jnp.dot(hits, first, preferred_element_type=f32)
        total = total + jnp.dot(hits, second, preferred_element_type=f32)
        return total + jnp.dot(hits, third, preferred_element_type=f32)

    out[...] = collect(me)

    @pl.loop(1, n)
    def _(o):
        term_copy(o).wait_recv()
        out[...] += collect(peer(o))

    @pl.loop(1, n)
    def _(o):
        id_copy(o).wait_send()
        latent_copy(1, o).wait_send()
        term_copy(o).wait_send()

    swap(0).wait_send()
    swap(1).wait_send()


def body(batch_ids, cond_ids, home, latent, diag_factor, cond_factor, obs, noise_prec):
    n = lax.axis_size("blk")
    per_owner, draws, width = latent.shape
    rows = batch_ids.shape[0]
    want = 4 * rows
    cap = max(2, 10 * rows // n)
    pad = -(-cap // 8) * 8
    block_ids = jnp.concatenate([batch_ids[:, None], cond_ids], axis=1).reshape(-1)
    wanted = home[block_ids].reshape(1, want)

    smem = pl.BlockSpec(memory_space=pltpu.SMEM)
    vmem = pl.BlockSpec(memory_space=pltpu.VMEM)
    anywhere = pl.BlockSpec(memory_space=pl.ANY)
    return pl.pallas_call(
        functools.partial(kernel, n, cap),
        out_shape=jax.ShapeDtypeStruct((per_owner, width // 2), f32),
        in_specs=[vmem, smem, anywhere, anywhere, anywhere, vmem],
        out_specs=vmem,
        scratch_shapes=[
            pltpu.VMEM((n, 1, want), jnp.int32),
            pltpu.VMEM((2 * n + 8, want), jnp.int32),
            pltpu.SMEM((2 * n + 8, want), jnp.int32),
            pltpu.VMEM(latent.shape, bf16),
            pltpu.VMEM((2, n, cap, draws, width // 2), bf16),
            pltpu.VMEM((n * cap, draws, width // 2), bf16),
            pltpu.VMEM((n * cap, draws, width // 2), bf16),
            pltpu.VMEM(diag_factor.shape, bf16),
            pltpu.VMEM(cond_factor.shape, bf16),
            pltpu.VMEM((rows, draws, width), f32),
            pltpu.VMEM((2, rows, width), f32),
            pltpu.VMEM((2, rows, width), f32),
            pltpu.VMEM((want, width // 2), f32),
            pltpu.VMEM((n, pad, width // 2), f32),
            pltpu.VMEM((n, pad, width // 2), f32),
            pltpu.SemaphoreType.DMA((4,)),
            pltpu.SemaphoreType.DMA((n,)),
            pltpu.SemaphoreType.DMA((n,)),
            pltpu.SemaphoreType.DMA((2 * n,)),
            pltpu.SemaphoreType.DMA((2 * n,)),
            pltpu.SemaphoreType.DMA((4,)),
            pltpu.SemaphoreType.DMA((n,)),
            pltpu.SemaphoreType.DMA((n,)),
        ],
        compiler_params=pltpu.CompilerParams(
            collective_id=0, has_side_effects=True, vmem_limit_bytes=56 * 1024 * 1024
        ),
    )(wanted, noise_prec.reshape(1), latent, diag_factor, cond_factor, obs)


def solution(mesh):
    placed = (
        P("blk"),
        P("blk", None),
        P(),
        P("blk", "mc", None),
        P("blk", None, None),
        P("blk", None, None, None),
        P("blk", None),
        P(),
    )
    return jax.shard_map(
        body, mesh=mesh, in_specs=placed, out_specs=P("blk", "mc"), check_vma=False
    )
```

```python
import functools

import jax
import jax.numpy as jnp
from jax import lax
from jax.experimental import pallas as pl
from jax.experimental.pallas import tpu as pltpu
from jax.sharding import PartitionSpec as P

freedom = 4.0
MESH = pl.DeviceIdType.MESH
f32 = jnp.float32
bf16 = jnp.bfloat16
NT = (((1,), (1,)), ((), ()))


def kernel(
    n,
    cap,
    batch_ids,
    cond_ids,
    home,
    noise,
    latent_any,
    diag,
    cond,
    obs,
    out,
    found,
    wanted,
    asked,
    every,
    tables,
    scalars,
    slots,
    flipped,
    hits,
    latent,
    outgoing,
    fetched_left,
    fetched_right,
    lower,
    near,
    partial,
    sums,
    sums_in,
    terms,
    outbox,
    inbox,
    load_sem,
    id_send,
    id_recv,
    lat_send,
    lat_recv,
    pair_sem,
    term_send,
    term_recv,
):
    fetched = (fetched_left, fetched_right)
    rows = obs.shape[0]
    want = 4 * rows
    per_owner, draws, width = latent.shape
    half = width // 2
    me = lax.axis_index("blk")
    core = lax.axis_index("mc")
    partner = (me, 1 - core)
    inverse_draws = 1.0 / (2 * draws)

    def peer(o):
        bit, other = 1, 0
        while bit < n:
            other = other + lax.rem(me // bit + o // bit, 2) * bit
            bit *= 2
        return other

    def turn(k):
        return lax.rem(k + 1, 2) * (n // 2) + (k + 1) // 2

    load_latent = pltpu.make_async_copy(latent_any, latent, load_sem.at[2])
    load_diag = pltpu.make_async_copy(diag, lower, load_sem.at[0])
    load_cond = pltpu.make_async_copy(cond, near, load_sem.at[1])
    load_latent.start()
    load_diag.start()
    load_cond.start()

    barrier = pltpu.get_barrier_semaphore()

    @pl.loop(1, n)
    def _(o):
        pl.semaphore_signal(
            barrier, inc=1, device_id=(peer(o), core), device_id_type=MESH
        )

    pl.semaphore_signal(barrier, inc=1, device_id=partner, device_id_type=MESH)

    @pl.loop(0, rows, unroll=8)
    def _(r):
        found[0, 4 * r] = home[batch_ids[r]]
        for k in range(3):
            found[0, 4 * r + k + 1] = home[cond_ids[k, r]]

    to_vector = pltpu.make_async_copy(found, wanted, load_sem.at[3])
    to_vector.start()
    to_vector.wait()

    lane = lax.broadcasted_iota(jnp.int32, (n, want), 1)
    owner = lax.broadcasted_iota(jnp.int32, (n, want), 0)
    slot = jnp.broadcast_to(wanted[...], (n, want)) - owner * per_owner
    mine = (slot >= 0) & (slot < per_owner)
    rank = jnp.where(mine, 1, 0)
    shift = 1
    while shift < want:
        rank = rank + jnp.where(lane >= shift, pltpu.roll(rank, shift, 1), 0)
        shift *= 2
    rank = jnp.where(mine, rank - 1, -1)

    def table(value):
        filled = jnp.zeros((n, want), jnp.int32)
        for c in range(cap):
            entry = jnp.sum(jnp.where(rank == c, value, 0), axis=1, keepdims=True)
            filled = jnp.where(lane == c, entry, filled)
        return filled

    asked[...] = (table(slot + 1) - 1).reshape(n, 1, want)
    pl.semaphore_wait(barrier, n)

    def id_copy(o):
        dst = peer(o)
        return pltpu.make_async_remote_copy(
            src_ref=asked.at[dst],
            dst_ref=every.at[me],
            send_sem=id_send.at[o],
            recv_sem=id_recv.at[o],
            device_id=(dst, core),
            device_id_type=MESH,
        )

    @pl.loop(1, n)
    def _(o):
        id_copy(o).start()

    every[me] = asked[me]
    tables[pl.ds(0, n)] = table(lane)
    spot = jnp.sum(jnp.where(mine, owner * cap + rank, 0), axis=0, keepdims=True)
    tables[pl.ds(n, 8)] = jnp.broadcast_to(spot, (8, want))
    to_scalars = pltpu.make_async_copy(tables, scalars, load_sem.at[3])
    to_scalars.start()

    @pl.loop(1, n)
    def _(o):
        id_copy(o).wait_recv()

    to_slots = pltpu.make_async_copy(every, slots, load_sem.at[4])
    to_slots.start()
    load_latent.wait()
    to_slots.wait()
    to_scalars.wait()

    def slot_of(owner, c):
        return jnp.maximum(slots[owner, 0, c], 0)

    def term_of(owner, c):
        return scalars[owner, c]

    def panel_of(w):
        return scalars[n, w]

    def latent_copy(h, o):
        dst = peer(o)
        return pltpu.make_async_remote_copy(
            src_ref=outgoing.at[h, dst],
            dst_ref=fetched[h].at[pl.ds(me * cap, cap)],
            send_sem=lat_send.at[h * n + o],
            recv_sem=lat_recv.at[h * n + o],
            device_id=(dst, core),
            device_id_type=MESH,
        )

    def pack(h, o):
        dst = peer(o)
        part = slice(h * half, (h + 1) * half)
        for c in range(cap):
            outgoing[h, dst, c] = latent[slot_of(dst, c), :, part]
        latent_copy(h, o).start()

    @pl.loop(0, n - 1)
    def _(k):
        pack(0, turn(k))

    for h in range(2):
        part = slice(h * half, (h + 1) * half)
        for c in range(cap):
            fetched[h][me * cap + c] = latent[slot_of(me, c), :, part]

    outbox[...] = jnp.zeros_like(outbox)
    pad = outbox.shape[1]
    load_diag.wait()
    load_cond.wait()
    keep = lax.broadcasted_iota(jnp.int32, (width, width), 0) >= lax.broadcasted_iota(
        jnp.int32, (width, width), 1
    )
    share = -(-rows // (n - 1))

    @pl.loop(0, n - 1)
    def _(k):
        for i in range(share):
            r = k * share + i

            @pl.when(r < rows)
            def _():
                lower[r] = jnp.where(keep, lower[r], jnp.zeros((width, width), bf16))
                flipped[r, pl.ds(0, half)] = lower[r, :, half:].T
                for j in range(3):
                    flipped[r, pl.ds((j + 1) * half, half)] = near[r, j, :, half:].T

        latent_copy(0, turn(k)).wait_send()
        pack(1, turn(k))

    position = lax.broadcasted_iota(jnp.int32, (per_owner, want), 0)
    spread = lax.broadcasted_iota(jnp.int32, (1, want), 1)

    @pl.loop(0, n)
    def _(source):
        row = every[source]
        row = jnp.where(spread < pad, row, -1)
        row = jnp.maximum(row, jnp.where(spread >= pad, pltpu.roll(row, pad, 1), -1))
        row = jnp.maximum(row, jnp.where(spread >= 2 * pad, pltpu.roll(row, pad, 1), -1))
        row = jnp.where(spread < 3 * pad, row, -1)
        hits[source] = jnp.where(position == row, 1.0, 0.0).astype(bf16)

    def panels(h, r):
        return jnp.concatenate([fetched[h][panel_of(4 * r + k)] for k in range(4)], axis=1)

    @pl.loop(1, n)
    def _(o):
        latent_copy(0, o).wait_recv()

    @pl.loop(0, rows, unroll=4)
    def _(r):
        blocks = [lower[r, :, :half]] + [near[r, k, :, :half] for k in range(3)]
        partial[r] = lax.dot_general(
            panels(0, r), jnp.concatenate(blocks, axis=1), NT, preferred_element_type=f32
        )

    @pl.loop(1, n)
    def _(o):
        latent_copy(1, o).wait_recv()

    group = rows // 2
    column = pl.ds(pl.multiple_of(core * half, half), half)
    place = lax.broadcasted_iota(jnp.int32, (16, width), 0)

    def swap(g):
        return pltpu.make_async_remote_copy(
            src_ref=sums.at[g],
            dst_ref=sums_in.at[g],
            send_sem=pair_sem.at[g],
            recv_sem=pair_sem.at[2 + g],
            device_id=partner,
            device_id_type=MESH,
        )

    for g in range(2):

        @pl.loop(0, group, unroll=4)
        def _(i):
            r = g * group + i
            white = partial[r] + jnp.dot(panels(1, r), flipped[r], preferred_element_type=f32)
            scored = (freedom + 1.0) * white / (freedom + white * white)
            low = scored.astype(bf16).astype(f32)
            sums[g, pl.ds(i, 1)] = jnp.sum(low, axis=0, keepdims=True)
            spot = panel_of(4 * r)
            own = jnp.concatenate([fetched_left[spot], fetched_right[spot]], axis=1).astype(f32)
            sums[g, pl.ds(group + i, 1)] = jnp.sum(own, axis=0, keepdims=True)

        swap(g).start()

    for g in range(2):
        swap(g).wait_recv()
        sums_in[g] = sums_in[g] + sums[g]

        @pl.loop(0, group, unroll=4)
        def _(i):
            r = g * group + i
            total = jnp.broadcast_to(sums_in[g, pl.ds(i, 1)], (16, width))
            high = total.astype(bf16).astype(f32)
            parts = jnp.where(place == 0, high, jnp.where(place == 1, total - high, 0.0)).astype(bf16)
            back = jnp.dot(parts, lower[r, :, column], preferred_element_type=f32)
            back = jnp.sum(back, axis=0, keepdims=True)
            own = sums_in[g, pl.ds(group + i, 1)]
            likely = noise[0] * (2 * draws * obs[pl.ds(r, 1)] - own)
            likely = jnp.where(core == 0, likely[:, :half], likely[:, half:])
            terms[pl.ds(4 * r, 1)] = (likely - back) * inverse_draws
            for k in range(3):
                back = jnp.dot(parts, near[r, k, :, column], preferred_element_type=f32)
                back = jnp.sum(back, axis=0, keepdims=True)
                terms[pl.ds(4 * r + k + 1, 1)] = -back * inverse_draws

    def term_copy(o):
        dst = peer(o)
        return pltpu.make_async_remote_copy(
            src_ref=outbox.at[dst],
            dst_ref=inbox.at[me],
            send_sem=term_send.at[o],
            recv_sem=term_recv.at[o],
            device_id=(dst, core),
            device_id_type=MESH,
        )

    @pl.loop(0, n - 1)
    def _(k):
        o = turn(k)
        dst = peer(o)
        for c in range(cap):
            outbox[dst, pl.ds(c, 1)] = terms[pl.ds(term_of(dst, c), 1)]
        term_copy(o).start()

    for c in range(cap):
        outbox[me, pl.ds(c, 1)] = terms[pl.ds(term_of(me, c), 1)]
    inbox[me] = outbox[me]

    def collect(source):
        arrived = inbox[source]
        first = arrived.astype(bf16)
        rest = arrived - first.astype(f32)
        second = rest.astype(bf16).astype(f32)
        parts = jnp.concatenate([first.astype(f32), second, rest - second], axis=0).astype(bf16)
        return jnp.dot(hits[source][:, : 3 * pad], parts, preferred_element_type=f32)

    out[...] = collect(me)

    @pl.loop(1, n)
    def _(o):
        term_copy(o).wait_recv()
        out[...] += collect(peer(o))

    @pl.loop(1, n)
    def _(o):
        id_copy(o).wait_send()
        latent_copy(1, o).wait_send()
        term_copy(o).wait_send()

    swap(0).wait_send()
    swap(1).wait_send()


def body(batch_ids, cond_ids, home, latent, diag_factor, cond_factor, obs, noise_prec):
    n = lax.axis_size("blk")
    per_owner, draws, width = latent.shape
    rows = batch_ids.shape[0]
    want = 4 * rows
    cap = max(2, 10 * rows // n)
    pad = -(-cap // 8) * 8
    smem = pl.BlockSpec(memory_space=pltpu.SMEM)
    vmem = pl.BlockSpec(memory_space=pltpu.VMEM)
    anywhere = pl.BlockSpec(memory_space=pl.ANY)
    return pl.pallas_call(
        functools.partial(kernel, n, cap),
        out_shape=jax.ShapeDtypeStruct((per_owner, width // 2), f32),
        in_specs=[smem, smem, smem, smem, anywhere, anywhere, anywhere, vmem],
        out_specs=vmem,
        scratch_shapes=[
            pltpu.SMEM((1, want), jnp.int32),
            pltpu.VMEM((1, want), jnp.int32),
            pltpu.VMEM((n, 1, want), jnp.int32),
            pltpu.VMEM((n, 1, want), jnp.int32),
            pltpu.VMEM((n + 8, want), jnp.int32),
            pltpu.SMEM((n + 8, want), jnp.int32),
            pltpu.SMEM((n, 1, want), jnp.int32),
            pltpu.VMEM((rows, 2 * width, width), bf16),
            pltpu.VMEM((n, per_owner, want), bf16),
            pltpu.VMEM(latent.shape, bf16),
            pltpu.VMEM((2, n, cap, draws, width // 2), bf16),
            pltpu.VMEM((n * cap, draws, width // 2), bf16),
            pltpu.VMEM((n * cap, draws, width // 2), bf16),
            pltpu.VMEM(diag_factor.shape, bf16),
            pltpu.VMEM(cond_factor.shape, bf16),
            pltpu.VMEM((rows, draws, width), f32),
            pltpu.VMEM((2, rows, width), f32),
            pltpu.VMEM((2, rows, width), f32),
            pltpu.VMEM((want, width // 2), f32),
            pltpu.VMEM((n, pad, width // 2), f32),
            pltpu.VMEM((n, pad, width // 2), f32),
            pltpu.SemaphoreType.DMA((5,)),
            pltpu.SemaphoreType.DMA((n,)),
            pltpu.SemaphoreType.DMA((n,)),
            pltpu.SemaphoreType.DMA((2 * n,)),
            pltpu.SemaphoreType.DMA((2 * n,)),
            pltpu.SemaphoreType.DMA((4,)),
            pltpu.SemaphoreType.DMA((n,)),
            pltpu.SemaphoreType.DMA((n,)),
        ],
        compiler_params=pltpu.CompilerParams(
            collective_id=0, has_side_effects=True, vmem_limit_bytes=56 * 1024 * 1024
        ),
    )(batch_ids, cond_ids.T, home, noise_prec.reshape(1), latent, diag_factor, cond_factor, obs)


def solution(mesh):
    placed = (
        P("blk"),
        P("blk", None),
        P(),
        P("blk", "mc", None),
        P("blk", None, None),
        P("blk", None, None, None),
        P("blk", None),
        P(),
    )
    return jax.shard_map(
        body, mesh=mesh, in_specs=placed, out_specs=P("blk", "mc"), check_vma=False
    )
```

```python
import functools

import jax
import jax.numpy as jnp
from jax import lax
from jax.experimental import pallas as pl
from jax.experimental.pallas import tpu as pltpu
from jax.sharding import PartitionSpec as P

freedom = 4.0
MESH = pl.DeviceIdType.MESH
f32 = jnp.float32
bf16 = jnp.bfloat16
NT = (((1,), (1,)), ((), ()))


def kernel(
    n,
    cap,
    batch_ids,
    cond_ids,
    home,
    noise,
    latent_any,
    diag,
    cond,
    obs,
    out,
    found,
    wanted,
    asked,
    every,
    tables,
    scalars,
    slots,
    flipped,
    hits,
    latent,
    outgoing,
    fetched_left,
    fetched_right,
    lower,
    near,
    partial,
    sums,
    sums_in,
    terms,
    outbox,
    inbox,
    load_sem,
    id_send,
    id_recv,
    lat_send,
    lat_recv,
    pair_sem,
    term_send,
    term_recv,
):
    fetched = (fetched_left, fetched_right)
    rows = obs.shape[0]
    want = 4 * rows
    per_owner, draws, width = latent.shape
    half = width // 2
    me = lax.axis_index("blk")
    core = lax.axis_index("mc")
    partner = (me, 1 - core)
    inverse_draws = 1.0 / (2 * draws)

    def peer(o):
        bit, other = 1, 0
        while bit < n:
            other = other + lax.rem(me // bit + o // bit, 2) * bit
            bit *= 2
        return other

    def turn(k):
        return lax.rem(k + 1, 2) * (n // 2) + (k + 1) // 2

    load_latent = pltpu.make_async_copy(latent_any, latent, load_sem.at[2])
    load_diag = pltpu.make_async_copy(diag, lower, load_sem.at[0])
    load_cond = pltpu.make_async_copy(cond, near, load_sem.at[1])
    load_latent.start()
    load_diag.start()
    load_cond.start()

    barrier = pltpu.get_barrier_semaphore()

    @pl.loop(1, n)
    def _(o):
        pl.semaphore_signal(
            barrier, inc=1, device_id=(peer(o), core), device_id_type=MESH
        )

    pl.semaphore_signal(barrier, inc=1, device_id=partner, device_id_type=MESH)

    @pl.loop(0, rows, unroll=8)
    def _(r):
        found[0, 4 * r] = home[batch_ids[r]]
        for k in range(3):
            found[0, 4 * r + k + 1] = home[cond_ids[k, r]]

    to_vector = pltpu.make_async_copy(found, wanted, load_sem.at[3])
    to_vector.start()
    to_vector.wait()

    lane = lax.broadcasted_iota(jnp.int32, (n, want), 1)
    owner = lax.broadcasted_iota(jnp.int32, (n, want), 0)
    slot = jnp.broadcast_to(wanted[...], (n, want)) - owner * per_owner
    mine = (slot >= 0) & (slot < per_owner)
    rank = jnp.where(mine, 1, 0)
    shift = 1
    while shift < want:
        rank = rank + jnp.where(lane >= shift, pltpu.roll(rank, shift, 1), 0)
        shift *= 2
    rank = jnp.where(mine, rank - 1, -1)

    def table(value):
        filled = jnp.zeros((n, want), jnp.int32)
        for c in range(cap):
            entry = jnp.sum(jnp.where(rank == c, value, 0), axis=1, keepdims=True)
            filled = jnp.where(lane == c, entry, filled)
        return filled

    asked[...] = (table(slot + 1) - 1).reshape(n, 1, want)
    pl.semaphore_wait(barrier, n)

    def id_copy(o):
        dst = peer(o)
        return pltpu.make_async_remote_copy(
            src_ref=asked.at[dst],
            dst_ref=every.at[me],
            send_sem=id_send.at[o],
            recv_sem=id_recv.at[o],
            device_id=(dst, core),
            device_id_type=MESH,
        )

    @pl.loop(1, n)
    def _(o):
        id_copy(o).start()

    every[me] = asked[me]
    tables[pl.ds(0, n)] = table(lane)
    spot = jnp.sum(jnp.where(mine, owner * cap + rank, 0), axis=0, keepdims=True)
    tables[pl.ds(n, 8)] = jnp.broadcast_to(spot, (8, want))
    to_scalars = pltpu.make_async_copy(tables, scalars, load_sem.at[3])
    to_scalars.start()

    @pl.loop(1, n)
    def _(o):
        id_copy(o).wait_recv()

    to_slots = pltpu.make_async_copy(every, slots, load_sem.at[4])
    to_slots.start()
    load_latent.wait()
    to_slots.wait()
    to_scalars.wait()

    def slot_of(owner, c):
        return jnp.maximum(slots[owner, 0, c], 0)

    def term_of(owner, c):
        return scalars[owner, c]

    def panel_of(w):
        return scalars[n, w]

    def latent_copy(h, o):
        dst = peer(o)
        return pltpu.make_async_remote_copy(
            src_ref=outgoing.at[h, dst],
            dst_ref=fetched[h].at[pl.ds(me * cap, cap)],
            send_sem=lat_send.at[h * n + o],
            recv_sem=lat_recv.at[h * n + o],
            device_id=(dst, core),
            device_id_type=MESH,
        )

    def pack(h, o):
        dst = peer(o)
        part = slice(h * half, (h + 1) * half)
        for c in range(cap):
            outgoing[h, dst, c] = latent[slot_of(dst, c), :, part]
        latent_copy(h, o).start()

    @pl.loop(0, n - 1)
    def _(k):
        pack(0, turn(k))

    for h in range(2):
        part = slice(h * half, (h + 1) * half)
        for c in range(cap):
            fetched[h][me * cap + c] = latent[slot_of(me, c), :, part]

    outbox[...] = jnp.zeros_like(outbox)
    pad = outbox.shape[1]
    load_diag.wait()
    load_cond.wait()
    keep = lax.broadcasted_iota(jnp.int32, (width, width), 0) >= lax.broadcasted_iota(
        jnp.int32, (width, width), 1
    )
    share = -(-rows // (n - 1))

    @pl.loop(0, n - 1)
    def _(k):
        for i in range(share):
            r = k * share + i

            @pl.when(r < rows)
            def _():
                lower[r] = jnp.where(keep, lower[r], jnp.zeros((width, width), bf16))

        latent_copy(0, turn(k)).wait_send()
        pack(1, turn(k))

    @pl.loop(0, rows)
    def _(r):
        flipped[r, pl.ds(0, half)] = lower[r, :, half:].T
        for j in range(3):
            flipped[r, pl.ds((j + 1) * half, half)] = near[r, j, :, half:].T

    position = lax.broadcasted_iota(jnp.int32, (per_owner, want), 0)
    spread = lax.broadcasted_iota(jnp.int32, (1, want), 1)

    @pl.loop(0, n)
    def _(source):
        row = every[source]
        row = jnp.where(spread < pad, row, -1)
        row = jnp.maximum(row, jnp.where(spread >= pad, pltpu.roll(row, pad, 1), -1))
        row = jnp.maximum(row, jnp.where(spread >= 2 * pad, pltpu.roll(row, pad, 1), -1))
        row = jnp.where(spread < 3 * pad, row, -1)
        hits[source] = jnp.where(position == row, 1.0, 0.0).astype(bf16)

    def panels(h, r):
        return jnp.concatenate([fetched[h][panel_of(4 * r + k)] for k in range(4)], axis=1)

    @pl.loop(1, n)
    def _(o):
        latent_copy(0, o).wait_recv()

    @pl.loop(0, rows, unroll=4)
    def _(r):
        blocks = [lower[r, :, :half]] + [near[r, k, :, :half] for k in range(3)]
        partial[r] = lax.dot_general(
            panels(0, r), jnp.concatenate(blocks, axis=1), NT, preferred_element_type=f32
        )

    @pl.loop(1, n)
    def _(o):
        latent_copy(1, o).wait_recv()

    group = rows // 2
    column = pl.ds(pl.multiple_of(core * half, half), half)
    place = lax.broadcasted_iota(jnp.int32, (16, width), 0)

    def swap(g):
        return pltpu.make_async_remote_copy(
            src_ref=sums.at[g],
            dst_ref=sums_in.at[g],
            send_sem=pair_sem.at[g],
            recv_sem=pair_sem.at[2 + g],
            device_id=partner,
            device_id_type=MESH,
        )

    for g in range(2):

        @pl.loop(0, group, unroll=8)
        def _(i):
            r = g * group + i
            white = partial[r] + jnp.dot(panels(1, r), flipped[r], preferred_element_type=f32)
            scored = (freedom + 1.0) * white / (freedom + white * white)
            low = scored.astype(bf16).astype(f32)
            sums[g, pl.ds(i, 1)] = jnp.sum(low, axis=0, keepdims=True)
            spot = panel_of(4 * r)
            own = jnp.concatenate([fetched_left[spot], fetched_right[spot]], axis=1).astype(f32)
            sums[g, pl.ds(group + i, 1)] = jnp.sum(own, axis=0, keepdims=True)

        swap(g).start()

    for g in range(2):
        swap(g).wait_recv()
        sums_in[g] = sums_in[g] + sums[g]

        @pl.loop(0, group, unroll=8)
        def _(i):
            r = g * group + i
            total = jnp.broadcast_to(sums_in[g, pl.ds(i, 1)], (16, width))
            high = total.astype(bf16).astype(f32)
            parts = jnp.where(place == 0, high, jnp.where(place == 1, total - high, 0.0)).astype(bf16)
            blocks = [lower[r, :, column]] + [near[r, k, :, column] for k in range(3)]
            back = jnp.dot(parts, jnp.concatenate(blocks, axis=1), preferred_element_type=f32)
            back = (back[0:1] + back[1:2]) * inverse_draws
            own = sums_in[g, pl.ds(group + i, 1)]
            likely = noise[0] * (2 * draws * obs[pl.ds(r, 1)] - own)
            likely = jnp.where(core == 0, likely[:, :half], likely[:, half:])
            terms[pl.ds(4 * r, 1)] = likely * inverse_draws - back[:, :half]
            for k in range(3):
                part = slice((k + 1) * half, (k + 2) * half)
                terms[pl.ds(4 * r + k + 1, 1)] = -back[:, part]

    def term_copy(o):
        dst = peer(o)
        return pltpu.make_async_remote_copy(
            src_ref=outbox.at[dst],
            dst_ref=inbox.at[me],
            send_sem=term_send.at[o],
            recv_sem=term_recv.at[o],
            device_id=(dst, core),
            device_id_type=MESH,
        )

    @pl.loop(0, n - 1)
    def _(k):
        o = turn(k)
        dst = peer(o)
        for c in range(cap):
            outbox[dst, pl.ds(c, 1)] = terms[pl.ds(term_of(dst, c), 1)]
        term_copy(o).start()

    for c in range(cap):
        outbox[me, pl.ds(c, 1)] = terms[pl.ds(term_of(me, c), 1)]
    inbox[me] = outbox[me]

    def collect(source):
        arrived = inbox[source]
        first = arrived.astype(bf16)
        rest = arrived - first.astype(f32)
        second = rest.astype(bf16).astype(f32)
        parts = jnp.concatenate([first.astype(f32), second, rest - second], axis=0).astype(bf16)
        return jnp.dot(hits[source][:, : 3 * pad], parts, preferred_element_type=f32)

    out[0] = collect(me)
    out[1] = jnp.zeros_like(out[1])

    @pl.loop(1, n)
    def _(o):
        term_copy(o).wait_recv()
        out[lax.rem(o, 2)] += collect(peer(o))

    @pl.loop(1, n)
    def _(o):
        id_copy(o).wait_send()
        latent_copy(1, o).wait_send()
        term_copy(o).wait_send()

    swap(0).wait_send()
    swap(1).wait_send()


def body(batch_ids, cond_ids, home, latent, diag_factor, cond_factor, obs, noise_prec):
    n = lax.axis_size("blk")
    per_owner, draws, width = latent.shape
    rows = batch_ids.shape[0]
    want = 4 * rows
    cap = max(2, 10 * rows // n)
    pad = -(-cap // 8) * 8
    smem = pl.BlockSpec(memory_space=pltpu.SMEM)
    vmem = pl.BlockSpec(memory_space=pltpu.VMEM)
    anywhere = pl.BlockSpec(memory_space=pl.ANY)
    partial_sums = pl.pallas_call(
        functools.partial(kernel, n, cap),
        out_shape=jax.ShapeDtypeStruct((2, per_owner, width // 2), f32),
        in_specs=[smem, smem, smem, smem, anywhere, anywhere, anywhere, vmem],
        out_specs=vmem,
        scratch_shapes=[
            pltpu.SMEM((1, want), jnp.int32),
            pltpu.VMEM((1, want), jnp.int32),
            pltpu.VMEM((n, 1, want), jnp.int32),
            pltpu.VMEM((n, 1, want), jnp.int32),
            pltpu.VMEM((n + 8, want), jnp.int32),
            pltpu.SMEM((n + 8, want), jnp.int32),
            pltpu.SMEM((n, 1, want), jnp.int32),
            pltpu.VMEM((rows, 2 * width, width), bf16),
            pltpu.VMEM((n, per_owner, want), bf16),
            pltpu.VMEM(latent.shape, bf16),
            pltpu.VMEM((2, n, cap, draws, width // 2), bf16),
            pltpu.VMEM((n * cap, draws, width // 2), bf16),
            pltpu.VMEM((n * cap, draws, width // 2), bf16),
            pltpu.VMEM(diag_factor.shape, bf16),
            pltpu.VMEM(cond_factor.shape, bf16),
            pltpu.VMEM((rows, draws, width), f32),
            pltpu.VMEM((2, rows, width), f32),
            pltpu.VMEM((2, rows, width), f32),
            pltpu.VMEM((want, width // 2), f32),
            pltpu.VMEM((n, pad, width // 2), f32),
            pltpu.VMEM((n, pad, width // 2), f32),
            pltpu.SemaphoreType.DMA((5,)),
            pltpu.SemaphoreType.DMA((n,)),
            pltpu.SemaphoreType.DMA((n,)),
            pltpu.SemaphoreType.DMA((2 * n,)),
            pltpu.SemaphoreType.DMA((2 * n,)),
            pltpu.SemaphoreType.DMA((4,)),
            pltpu.SemaphoreType.DMA((n,)),
            pltpu.SemaphoreType.DMA((n,)),
        ],
        compiler_params=pltpu.CompilerParams(
            collective_id=0, has_side_effects=True, vmem_limit_bytes=56 * 1024 * 1024
        ),
    )(batch_ids, cond_ids.T, home, noise_prec.reshape(1), latent, diag_factor, cond_factor, obs)
    return partial_sums[0] + partial_sums[1]


def solution(mesh):
    placed = (
        P("blk"),
        P("blk", None),
        P(),
        P("blk", "mc", None),
        P("blk", None, None),
        P("blk", None, None, None),
        P("blk", None),
        P(),
    )
    return jax.shard_map(
        body, mesh=mesh, in_specs=placed, out_specs=P("blk", "mc"), check_vma=False
    )
```

```python
import functools

import jax
import jax.numpy as jnp
from jax import lax
from jax.experimental import pallas as pl
from jax.experimental.pallas import tpu as pltpu
from jax.sharding import PartitionSpec as P

freedom = 4.0
MESH = pl.DeviceIdType.MESH
f32 = jnp.float32
bf16 = jnp.bfloat16
NT = (((1,), (1,)), ((), ()))


def kernel(
    n,
    cap,
    batch_ids,
    cond_ids,
    home,
    noise,
    latent_any,
    diag,
    cond,
    obs,
    out,
    found,
    wanted,
    asked,
    every,
    tables,
    scalars,
    slots,
    flipped,
    hits,
    latent,
    outgoing,
    fetched_left,
    fetched_right,
    lower,
    near,
    partial,
    sums,
    sums_in,
    terms,
    outbox,
    inbox,
    load_sem,
    id_send,
    id_recv,
    lat_send,
    lat_recv,
    pair_sem,
    term_send,
    term_recv,
):
    fetched = (fetched_left, fetched_right)
    rows = obs.shape[0]
    want = 4 * rows
    per_owner, draws, width = latent.shape
    half = width // 2
    me = lax.axis_index("blk")
    core = lax.axis_index("mc")
    partner = (me, 1 - core)
    inverse_draws = 1.0 / (2 * draws)

    def peer(o):
        bit, other = 1, 0
        while bit < n:
            other = other + lax.rem(me // bit + o // bit, 2) * bit
            bit *= 2
        return other

    def turn(k):
        return lax.rem(k + 1, 2) * (n // 2) + (k + 1) // 2

    load_latent = pltpu.make_async_copy(latent_any, latent, load_sem.at[2])
    load_diag = pltpu.make_async_copy(diag, lower, load_sem.at[0])
    load_cond = pltpu.make_async_copy(cond, near, load_sem.at[1])
    load_latent.start()

    barrier = pltpu.get_barrier_semaphore()

    @pl.loop(1, n)
    def _(o):
        pl.semaphore_signal(
            barrier, inc=1, device_id=(peer(o), core), device_id_type=MESH
        )

    pl.semaphore_signal(barrier, inc=1, device_id=partner, device_id_type=MESH)

    @pl.loop(0, rows, unroll=8)
    def _(r):
        found[0, 4 * r] = home[batch_ids[r]]
        for k in range(3):
            found[0, 4 * r + k + 1] = home[cond_ids[k, r]]

    to_vector = pltpu.make_async_copy(found, wanted, load_sem.at[3])
    to_vector.start()
    to_vector.wait()

    lane = lax.broadcasted_iota(jnp.int32, (n, want), 1)
    owner = lax.broadcasted_iota(jnp.int32, (n, want), 0)
    slot = jnp.broadcast_to(wanted[...], (n, want)) - owner * per_owner
    mine = (slot >= 0) & (slot < per_owner)
    rank = jnp.where(mine, 1, 0)
    shift = 1
    while shift < want:
        rank = rank + jnp.where(lane >= shift, pltpu.roll(rank, shift, 1), 0)
        shift *= 2
    rank = jnp.where(mine, rank - 1, -1)

    def table(value):
        filled = jnp.zeros((n, want), jnp.int32)
        for c in range(cap):
            entry = jnp.sum(jnp.where(rank == c, value, 0), axis=1, keepdims=True)
            filled = jnp.where(lane == c, entry, filled)
        return filled

    asked[...] = (table(slot + 1) - 1).reshape(n, 1, want)
    pl.semaphore_wait(barrier, n)

    def id_copy(o):
        dst = peer(o)
        return pltpu.make_async_remote_copy(
            src_ref=asked.at[dst],
            dst_ref=every.at[me],
            send_sem=id_send.at[o],
            recv_sem=id_recv.at[o],
            device_id=(dst, core),
            device_id_type=MESH,
        )

    @pl.loop(1, n)
    def _(o):
        id_copy(o).start()

    every[me] = asked[me]
    tables[pl.ds(0, n)] = table(lane)
    spot = jnp.sum(jnp.where(mine, owner * cap + rank, 0), axis=0, keepdims=True)
    tables[pl.ds(n, 8)] = jnp.broadcast_to(spot, (8, want))
    to_scalars = pltpu.make_async_copy(tables, scalars, load_sem.at[3])
    to_scalars.start()

    @pl.loop(1, n)
    def _(o):
        id_copy(o).wait_recv()

    to_slots = pltpu.make_async_copy(every, slots, load_sem.at[4])
    to_slots.start()
    load_latent.wait()
    to_slots.wait()
    to_scalars.wait()

    def slot_of(owner, c):
        return jnp.maximum(slots[owner, 0, c], 0)

    def term_of(owner, c):
        return scalars[owner, c]

    def panel_of(w):
        return scalars[n, w]

    def latent_copy(h, o):
        dst = peer(o)
        return pltpu.make_async_remote_copy(
            src_ref=outgoing.at[h, dst],
            dst_ref=fetched[h].at[pl.ds(me * cap, cap)],
            send_sem=lat_send.at[h * n + o],
            recv_sem=lat_recv.at[h * n + o],
            device_id=(dst, core),
            device_id_type=MESH,
        )

    def pack(h, o):
        dst = peer(o)
        part = slice(h * half, (h + 1) * half)
        for c in range(cap):
            outgoing[h, dst, c] = latent[slot_of(dst, c), :, part]

    @pl.loop(0, n - 1)
    def _(k):
        pack(0, turn(k))
        latent_copy(0, turn(k)).start()

    lead = n // 4

    @pl.loop(0, lead)
    def _(k):
        pack(1, n // 2 + k)
        latent_copy(1, n // 2 + k).start()

    load_diag.start()
    load_cond.start()

    @pl.loop(0, n - 1)
    def _(k):
        o = turn(k)

        @pl.when((o < n // 2) | (o >= n // 2 + lead))
        def _():
            pack(1, o)

    for h in range(2):
        part = slice(h * half, (h + 1) * half)
        for c in range(cap):
            fetched[h][me * cap + c] = latent[slot_of(me, c), :, part]

    outbox[...] = jnp.zeros_like(outbox)
    pad = outbox.shape[1]
    load_diag.wait()
    load_cond.wait()
    keep = lax.broadcasted_iota(jnp.int32, (width, width), 0) >= lax.broadcasted_iota(
        jnp.int32, (width, width), 1
    )
    share = -(-rows // (n - 1))

    @pl.loop(0, n - 1)
    def _(k):
        for i in range(share):
            r = k * share + i

            @pl.when(r < rows)
            def _():
                lower[r] = jnp.where(keep, lower[r], jnp.zeros((width, width), bf16))

        o = turn(k)
        latent_copy(0, o).wait_send()

        @pl.when((o < n // 2) | (o >= n // 2 + lead))
        def _():
            latent_copy(1, o).start()

    @pl.loop(0, rows)
    def _(r):
        flipped[r, pl.ds(0, half)] = lower[r, :, half:].T
        for j in range(3):
            flipped[r, pl.ds((j + 1) * half, half)] = near[r, j, :, half:].T

    position = lax.broadcasted_iota(jnp.int32, (per_owner, want), 0)
    spread = lax.broadcasted_iota(jnp.int32, (1, want), 1)

    @pl.loop(0, n)
    def _(source):
        row = every[source]
        row = jnp.where(spread < pad, row, -1)
        row = jnp.maximum(row, jnp.where(spread >= pad, pltpu.roll(row, pad, 1), -1))
        row = jnp.maximum(row, jnp.where(spread >= 2 * pad, pltpu.roll(row, pad, 1), -1))
        row = jnp.where(spread < 3 * pad, row, -1)
        hits[source] = jnp.where(position == row, 1.0, 0.0).astype(bf16)

    def panels(h, r):
        return jnp.concatenate([fetched[h][panel_of(4 * r + k)] for k in range(4)], axis=1)

    @pl.loop(1, n)
    def _(o):
        latent_copy(0, o).wait_recv()

    @pl.loop(0, rows, unroll=4)
    def _(r):
        blocks = [lower[r, :, :half]] + [near[r, k, :, :half] for k in range(3)]
        partial[r] = lax.dot_general(
            panels(0, r), jnp.concatenate(blocks, axis=1), NT, preferred_element_type=f32
        )

    @pl.loop(1, n)
    def _(o):
        latent_copy(1, o).wait_recv()

    group = rows // 2
    column = pl.ds(pl.multiple_of(core * half, half), half)
    place = lax.broadcasted_iota(jnp.int32, (16, width), 0)

    def swap(g):
        return pltpu.make_async_remote_copy(
            src_ref=sums.at[g],
            dst_ref=sums_in.at[g],
            send_sem=pair_sem.at[g],
            recv_sem=pair_sem.at[2 + g],
            device_id=partner,
            device_id_type=MESH,
        )

    for g in range(2):

        @pl.loop(0, group, unroll=8)
        def _(i):
            r = g * group + i
            white = partial[r] + jnp.dot(panels(1, r), flipped[r], preferred_element_type=f32)
            scored = (freedom + 1.0) * white / (freedom + white * white)
            low = scored.astype(bf16).astype(f32)
            sums[g, pl.ds(i, 1)] = jnp.sum(low, axis=0, keepdims=True)
            spot = panel_of(4 * r)
            own = jnp.concatenate([fetched_left[spot], fetched_right[spot]], axis=1).astype(f32)
            sums[g, pl.ds(group + i, 1)] = jnp.sum(own, axis=0, keepdims=True)

        swap(g).start()

    for g in range(2):
        swap(g).wait_recv()
        sums_in[g] = sums_in[g] + sums[g]

        @pl.loop(0, group, unroll=8)
        def _(i):
            r = g * group + i
            total = jnp.broadcast_to(sums_in[g, pl.ds(i, 1)], (16, width))
            high = total.astype(bf16).astype(f32)
            parts = jnp.where(place == 0, high, jnp.where(place == 1, total - high, 0.0)).astype(bf16)
            blocks = [lower[r, :, column]] + [near[r, k, :, column] for k in range(3)]
            back = jnp.dot(parts, jnp.concatenate(blocks, axis=1), preferred_element_type=f32)
            back = (back[0:1] + back[1:2]) * inverse_draws
            own = sums_in[g, pl.ds(group + i, 1)]
            likely = noise[0] * (2 * draws * obs[pl.ds(r, 1)] - own)
            likely = jnp.where(core == 0, likely[:, :half], likely[:, half:])
            terms[pl.ds(4 * r, 1)] = likely * inverse_draws - back[:, :half]
            for k in range(3):
                part = slice((k + 1) * half, (k + 2) * half)
                terms[pl.ds(4 * r + k + 1, 1)] = -back[:, part]

    def term_copy(o):
        dst = peer(o)
        return pltpu.make_async_remote_copy(
            src_ref=outbox.at[dst],
            dst_ref=inbox.at[me],
            send_sem=term_send.at[o],
            recv_sem=term_recv.at[o],
            device_id=(dst, core),
            device_id_type=MESH,
        )

    @pl.loop(0, n - 1)
    def _(k):
        o = turn(k)
        dst = peer(o)
        for c in range(cap):
            outbox[dst, pl.ds(c, 1)] = terms[pl.ds(term_of(dst, c), 1)]
        term_copy(o).start()

    for c in range(cap):
        outbox[me, pl.ds(c, 1)] = terms[pl.ds(term_of(me, c), 1)]
    inbox[me] = outbox[me]

    def collect(source):
        arrived = inbox[source]
        first = arrived.astype(bf16)
        rest = arrived - first.astype(f32)
        second = rest.astype(bf16).astype(f32)
        parts = jnp.concatenate([first.astype(f32), second, rest - second], axis=0).astype(bf16)
        return jnp.dot(hits[source][:, : 3 * pad], parts, preferred_element_type=f32)

    out[0] = collect(me)
    out[1] = jnp.zeros_like(out[1])

    @pl.loop(1, n)
    def _(o):
        term_copy(o).wait_recv()
        out[lax.rem(o, 2)] += collect(peer(o))

    @pl.loop(1, n)
    def _(o):
        id_copy(o).wait_send()
        latent_copy(1, o).wait_send()
        term_copy(o).wait_send()

    swap(0).wait_send()
    swap(1).wait_send()


def body(batch_ids, cond_ids, home, latent, diag_factor, cond_factor, obs, noise_prec):
    n = lax.axis_size("blk")
    per_owner, draws, width = latent.shape
    rows = batch_ids.shape[0]
    want = 4 * rows
    cap = max(2, 10 * rows // n)
    pad = -(-cap // 8) * 8
    smem = pl.BlockSpec(memory_space=pltpu.SMEM)
    vmem = pl.BlockSpec(memory_space=pltpu.VMEM)
    anywhere = pl.BlockSpec(memory_space=pl.ANY)
    partial_sums = pl.pallas_call(
        functools.partial(kernel, n, cap),
        out_shape=jax.ShapeDtypeStruct((2, per_owner, width // 2), f32),
        in_specs=[smem, smem, smem, smem, anywhere, anywhere, anywhere, vmem],
        out_specs=vmem,
        scratch_shapes=[
            pltpu.SMEM((1, want), jnp.int32),
            pltpu.VMEM((1, want), jnp.int32),
            pltpu.VMEM((n, 1, want), jnp.int32),
            pltpu.VMEM((n, 1, want), jnp.int32),
            pltpu.VMEM((n + 8, want), jnp.int32),
            pltpu.SMEM((n + 8, want), jnp.int32),
            pltpu.SMEM((n, 1, want), jnp.int32),
            pltpu.VMEM((rows, 2 * width, width), bf16),
            pltpu.VMEM((n, per_owner, want), bf16),
            pltpu.VMEM(latent.shape, bf16),
            pltpu.VMEM((2, n, cap, draws, width // 2), bf16),
            pltpu.VMEM((n * cap, draws, width // 2), bf16),
            pltpu.VMEM((n * cap, draws, width // 2), bf16),
            pltpu.VMEM(diag_factor.shape, bf16),
            pltpu.VMEM(cond_factor.shape, bf16),
            pltpu.VMEM((rows, draws, width), f32),
            pltpu.VMEM((2, rows, width), f32),
            pltpu.VMEM((2, rows, width), f32),
            pltpu.VMEM((want, width // 2), f32),
            pltpu.VMEM((n, pad, width // 2), f32),
            pltpu.VMEM((n, pad, width // 2), f32),
            pltpu.SemaphoreType.DMA((5,)),
            pltpu.SemaphoreType.DMA((n,)),
            pltpu.SemaphoreType.DMA((n,)),
            pltpu.SemaphoreType.DMA((2 * n,)),
            pltpu.SemaphoreType.DMA((2 * n,)),
            pltpu.SemaphoreType.DMA((4,)),
            pltpu.SemaphoreType.DMA((n,)),
            pltpu.SemaphoreType.DMA((n,)),
        ],
        compiler_params=pltpu.CompilerParams(
            collective_id=0, has_side_effects=True, vmem_limit_bytes=56 * 1024 * 1024
        ),
    )(batch_ids, cond_ids.T, home, noise_prec.reshape(1), latent, diag_factor, cond_factor, obs)
    return partial_sums[0] + partial_sums[1]


def solution(mesh):
    placed = (
        P("blk"),
        P("blk", None),
        P(),
        P("blk", "mc", None),
        P("blk", None, None),
        P("blk", None, None, None),
        P("blk", None),
        P(),
    )
    return jax.shard_map(
        body, mesh=mesh, in_specs=placed, out_specs=P("blk", "mc"), check_vma=False
    )
```

```python
import functools

import jax
import jax.numpy as jnp
from jax import lax
from jax.experimental import pallas as pl
from jax.experimental.pallas import tpu as pltpu
from jax.sharding import PartitionSpec as P

freedom = 4.0
MESH = pl.DeviceIdType.MESH
f32 = jnp.float32
bf16 = jnp.bfloat16
NT = (((1,), (1,)), ((), ()))


def kernel(
    n,
    cap,
    batch_ids,
    cond_ids,
    home,
    noise,
    latent_any,
    diag,
    cond,
    obs,
    out,
    asked,
    every,
    tables,
    scalars,
    slots,
    flipped,
    hits,
    latent,
    outgoing,
    fetched_left,
    fetched_right,
    lower,
    near,
    partial,
    sums,
    sums_in,
    terms,
    outbox,
    inbox,
    load_sem,
    id_send,
    id_recv,
    lat_send,
    lat_recv,
    pair_sem,
    term_send,
    term_recv,
):
    fetched = (fetched_left, fetched_right)
    rows = obs.shape[0]
    want = 4 * rows
    per_owner, draws, width = latent.shape
    half = width // 2
    me = lax.axis_index("blk")
    core = lax.axis_index("mc")
    partner = (me, 1 - core)
    inverse_draws = 1.0 / (2 * draws)

    def peer(o):
        bit, other = 1, 0
        while bit < n:
            other = other + lax.rem(me // bit + o // bit, 2) * bit
            bit *= 2
        return other

    def turn(k):
        return lax.rem(k + 1, 2) * (n // 2) + (k + 1) // 2

    load_latent = pltpu.make_async_copy(latent_any, latent, load_sem.at[2])
    load_diag = pltpu.make_async_copy(diag, lower, load_sem.at[0])
    load_cond = pltpu.make_async_copy(cond, near, load_sem.at[1])
    load_latent.start()

    barrier = pltpu.get_barrier_semaphore()

    @pl.loop(1, n)
    def _(o):
        pl.semaphore_signal(
            barrier, inc=1, device_id=(peer(o), core), device_id_type=MESH
        )

    pl.semaphore_signal(barrier, inc=1, device_id=partner, device_id_type=MESH)

    entry_lane = lax.broadcasted_iota(jnp.int32, (8, want), 1)

    def look_up(r, known):
        known = jnp.where(entry_lane == 4 * r, home[batch_ids[r]], known)
        for k in range(3):
            known = jnp.where(entry_lane == 4 * r + k + 1, home[cond_ids[k, r]], known)
        return known

    wanted = lax.fori_loop(0, rows, look_up, jnp.zeros((8, want), jnp.int32), unroll=8)
    lane = lax.broadcasted_iota(jnp.int32, (n, want), 1)
    owner = lax.broadcasted_iota(jnp.int32, (n, want), 0)
    slot = jnp.broadcast_to(wanted[0:1], (n, want)) - owner * per_owner
    mine = (slot >= 0) & (slot < per_owner)
    rank = jnp.where(mine, 1, 0)
    shift = 1
    while shift < want:
        rank = rank + jnp.where(lane >= shift, pltpu.roll(rank, shift, 1), 0)
        shift *= 2
    rank = jnp.where(mine, rank - 1, -1)

    def table(value):
        filled = jnp.zeros((n, want), jnp.int32)
        for c in range(cap):
            entry = jnp.sum(jnp.where(rank == c, value, 0), axis=1, keepdims=True)
            filled = jnp.where(lane == c, entry, filled)
        return filled

    asked[...] = (table(slot + 1) - 1).reshape(n, 1, want)
    pl.semaphore_wait(barrier, n)

    def id_copy(o):
        dst = peer(o)
        return pltpu.make_async_remote_copy(
            src_ref=asked.at[dst],
            dst_ref=every.at[me],
            send_sem=id_send.at[o],
            recv_sem=id_recv.at[o],
            device_id=(dst, core),
            device_id_type=MESH,
        )

    @pl.loop(1, n)
    def _(o):
        id_copy(o).start()

    every[me] = asked[me]
    tables[pl.ds(0, n)] = table(lane)
    spot = jnp.sum(jnp.where(mine, owner * cap + rank, 0), axis=0, keepdims=True)
    tables[pl.ds(n, 8)] = jnp.broadcast_to(spot, (8, want))
    to_scalars = pltpu.make_async_copy(tables, scalars, load_sem.at[3])
    to_scalars.start()

    @pl.loop(1, n)
    def _(o):
        id_copy(o).wait_recv()

    to_slots = pltpu.make_async_copy(every, slots, load_sem.at[4])
    to_slots.start()
    load_latent.wait()
    to_slots.wait()
    to_scalars.wait()

    def slot_of(owner, c):
        return jnp.maximum(slots[owner, 0, c], 0)

    def term_of(owner, c):
        return scalars[owner, c]

    def panel_of(w):
        return scalars[n, w]

    def latent_copy(h, o):
        dst = peer(o)
        return pltpu.make_async_remote_copy(
            src_ref=outgoing.at[h, dst],
            dst_ref=fetched[h].at[pl.ds(me * cap, cap)],
            send_sem=lat_send.at[h * n + o],
            recv_sem=lat_recv.at[h * n + o],
            device_id=(dst, core),
            device_id_type=MESH,
        )

    def pack(h, o):
        dst = peer(o)
        part = slice(h * half, (h + 1) * half)
        for c in range(cap):
            outgoing[h, dst, c] = latent[slot_of(dst, c), :, part]

    @pl.loop(0, n - 1)
    def _(k):
        pack(0, turn(k))
        latent_copy(0, turn(k)).start()

    lead = n // 4

    @pl.loop(0, lead)
    def _(k):
        pack(1, n // 2 + k)
        latent_copy(1, n // 2 + k).start()

    load_diag.start()
    load_cond.start()

    @pl.loop(0, n - 1)
    def _(k):
        o = turn(k)

        @pl.when((o < n // 2) | (o >= n // 2 + lead))
        def _():
            pack(1, o)

    for h in range(2):
        part = slice(h * half, (h + 1) * half)
        for c in range(cap):
            fetched[h][me * cap + c] = latent[slot_of(me, c), :, part]

    pad = -(-cap // 8) * 8
    load_diag.wait()
    load_cond.wait()
    keep = lax.broadcasted_iota(jnp.int32, (width, width), 0) >= lax.broadcasted_iota(
        jnp.int32, (width, width), 1
    )
    share = -(-rows // (n - 1))

    @pl.loop(0, n - 1)
    def _(k):
        for i in range(share):
            r = k * share + i

            @pl.when(r < rows)
            def _():
                lower[r] = jnp.where(keep, lower[r], jnp.zeros((width, width), bf16))

        o = turn(k)
        latent_copy(0, o).wait_send()

        @pl.when((o < n // 2) | (o >= n // 2 + lead))
        def _():
            latent_copy(1, o).start()

    @pl.loop(0, rows)
    def _(r):
        flipped[r, pl.ds(0, half)] = lower[r, :, half:].T
        for j in range(3):
            flipped[r, pl.ds((j + 1) * half, half)] = near[r, j, :, half:].T

    position = lax.broadcasted_iota(jnp.int32, (per_owner, want), 0)
    spread = lax.broadcasted_iota(jnp.int32, (1, want), 1)

    @pl.loop(0, n)
    def _(source):
        row = every[source]
        row = jnp.where(spread < pad, row, -1)
        row = jnp.maximum(row, jnp.where(spread >= pad, pltpu.roll(row, pad, 1), -1))
        row = jnp.maximum(row, jnp.where(spread >= 2 * pad, pltpu.roll(row, pad, 1), -1))
        row = jnp.where(spread < 3 * pad, row, -1)
        hits[source] = jnp.where(position == row, 1.0, 0.0).astype(bf16)

    def panels(h, r):
        return jnp.concatenate([fetched[h][panel_of(4 * r + k)] for k in range(4)], axis=1)

    @pl.loop(1, n)
    def _(o):
        latent_copy(0, o).wait_recv()

    @pl.loop(0, rows, unroll=4)
    def _(r):
        blocks = [lower[r, :, :half]] + [near[r, k, :, :half] for k in range(3)]
        partial[r] = lax.dot_general(
            panels(0, r), jnp.concatenate(blocks, axis=1), NT, preferred_element_type=f32
        )

    @pl.loop(1, n)
    def _(o):
        latent_copy(1, o).wait_recv()

    group = rows // 2
    column = pl.ds(pl.multiple_of(core * half, half), half)
    place = lax.broadcasted_iota(jnp.int32, (16, width), 0)

    def swap(g):
        return pltpu.make_async_remote_copy(
            src_ref=sums.at[g],
            dst_ref=sums_in.at[g],
            send_sem=pair_sem.at[g],
            recv_sem=pair_sem.at[2 + g],
            device_id=partner,
            device_id_type=MESH,
        )

    for g in range(2):

        @pl.loop(0, group, unroll=8)
        def _(i):
            r = g * group + i
            white = partial[r] + jnp.dot(panels(1, r), flipped[r], preferred_element_type=f32)
            scored = (freedom + 1.0) * white / (freedom + white * white)
            low = scored.astype(bf16).astype(f32)
            sums[g, pl.ds(i, 1)] = jnp.sum(low, axis=0, keepdims=True)
            spot = panel_of(4 * r)
            own = jnp.concatenate([fetched_left[spot], fetched_right[spot]], axis=1).astype(f32)
            sums[g, pl.ds(group + i, 1)] = jnp.sum(own, axis=0, keepdims=True)

        swap(g).start()

    for g in range(2):
        swap(g).wait_recv()
        sums_in[g] = sums_in[g] + sums[g]

        @pl.loop(0, group, unroll=8)
        def _(i):
            r = g * group + i
            total = jnp.broadcast_to(sums_in[g, pl.ds(i, 1)], (16, width))
            high = total.astype(bf16).astype(f32)
            parts = jnp.where(place == 0, high, jnp.where(place == 1, total - high, 0.0)).astype(bf16)
            blocks = [lower[r, :, column]] + [near[r, k, :, column] for k in range(3)]
            back = jnp.dot(parts, jnp.concatenate(blocks, axis=1), preferred_element_type=f32)
            back = (back[0:1] + back[1:2]) * inverse_draws
            own = sums_in[g, pl.ds(group + i, 1)]
            likely = noise[0] * (2 * draws * obs[pl.ds(r, 1)] - own)
            likely = jnp.where(core == 0, likely[:, :half], likely[:, half:])
            terms[pl.ds(4 * r, 1)] = likely * inverse_draws - back[:, :half]
            for k in range(3):
                part = slice((k + 1) * half, (k + 2) * half)
                terms[pl.ds(4 * r + k + 1, 1)] = -back[:, part]

    def term_copy(o):
        dst = peer(o)
        return pltpu.make_async_remote_copy(
            src_ref=outbox.at[dst],
            dst_ref=inbox.at[me],
            send_sem=term_send.at[o],
            recv_sem=term_recv.at[o],
            device_id=(dst, core),
            device_id_type=MESH,
        )

    @pl.loop(0, n - 1)
    def _(k):
        o = turn(k)
        dst = peer(o)
        for c in range(cap):
            outbox[dst, pl.ds(c, 1)] = terms[pl.ds(term_of(dst, c), 1)]
        term_copy(o).start()

    for c in range(cap):
        outbox[me, pl.ds(c, 1)] = terms[pl.ds(term_of(me, c), 1)]
    inbox[me] = outbox[me]

    def collect(source):
        blank = jnp.zeros((pad - cap, half), f32)
        arrived = jnp.concatenate([inbox[source], blank], axis=0) if pad > cap else inbox[source]
        first = arrived.astype(bf16)
        rest = arrived - first.astype(f32)
        second = rest.astype(bf16).astype(f32)
        parts = jnp.concatenate([first.astype(f32), second, rest - second], axis=0).astype(bf16)
        return jnp.dot(hits[source][:, : 3 * pad], parts, preferred_element_type=f32)

    out[0] = collect(me)
    out[1] = jnp.zeros_like(out[1])

    @pl.loop(1, n)
    def _(o):
        term_copy(o).wait_recv()
        out[lax.rem(o, 2)] += collect(peer(o))

    @pl.loop(1, n)
    def _(o):
        id_copy(o).wait_send()
        latent_copy(1, o).wait_send()
        term_copy(o).wait_send()

    swap(0).wait_send()
    swap(1).wait_send()


def body(batch_ids, cond_ids, home, latent, diag_factor, cond_factor, obs, noise_prec):
    n = lax.axis_size("blk")
    per_owner, draws, width = latent.shape
    rows = batch_ids.shape[0]
    want = 4 * rows
    cap = max(2, 10 * rows // n)
    smem = pl.BlockSpec(memory_space=pltpu.SMEM)
    vmem = pl.BlockSpec(memory_space=pltpu.VMEM)
    anywhere = pl.BlockSpec(memory_space=pl.ANY)
    partial_sums = pl.pallas_call(
        functools.partial(kernel, n, cap),
        out_shape=jax.ShapeDtypeStruct((2, per_owner, width // 2), f32),
        in_specs=[smem, smem, smem, smem, anywhere, anywhere, anywhere, vmem],
        out_specs=vmem,
        scratch_shapes=[
            pltpu.VMEM((n, 1, want), jnp.int32),
            pltpu.VMEM((n, 1, want), jnp.int32),
            pltpu.VMEM((n + 8, want), jnp.int32),
            pltpu.SMEM((n + 8, want), jnp.int32),
            pltpu.SMEM((n, 1, want), jnp.int32),
            pltpu.VMEM((rows, 2 * width, width), bf16),
            pltpu.VMEM((n, per_owner, want), bf16),
            pltpu.VMEM(latent.shape, bf16),
            pltpu.VMEM((2, n, cap, draws, width // 2), bf16),
            pltpu.VMEM((n * cap, draws, width // 2), bf16),
            pltpu.VMEM((n * cap, draws, width // 2), bf16),
            pltpu.VMEM(diag_factor.shape, bf16),
            pltpu.VMEM(cond_factor.shape, bf16),
            pltpu.VMEM((rows, draws, width), f32),
            pltpu.VMEM((2, rows, width), f32),
            pltpu.VMEM((2, rows, width), f32),
            pltpu.VMEM((want, width // 2), f32),
            pltpu.VMEM((n, cap, width // 2), f32),
            pltpu.VMEM((n, cap, width // 2), f32),
            pltpu.SemaphoreType.DMA((5,)),
            pltpu.SemaphoreType.DMA((n,)),
            pltpu.SemaphoreType.DMA((n,)),
            pltpu.SemaphoreType.DMA((2 * n,)),
            pltpu.SemaphoreType.DMA((2 * n,)),
            pltpu.SemaphoreType.DMA((4,)),
            pltpu.SemaphoreType.DMA((n,)),
            pltpu.SemaphoreType.DMA((n,)),
        ],
        compiler_params=pltpu.CompilerParams(
            collective_id=0, has_side_effects=True, vmem_limit_bytes=56 * 1024 * 1024
        ),
    )(batch_ids, cond_ids.T, home, noise_prec.reshape(1), latent, diag_factor, cond_factor, obs)
    return partial_sums[0] + partial_sums[1]


def solution(mesh):
    placed = (
        P("blk"),
        P("blk", None),
        P(),
        P("blk", "mc", None),
        P("blk", None, None),
        P("blk", None, None, None),
        P("blk", None),
        P(),
    )
    return jax.shard_map(
        body, mesh=mesh, in_specs=placed, out_specs=P("blk", "mc"), check_vma=False
    )
```
